256 devices in a mesh: quartet: 128 (over z, y, x), pert: 2 (over core).
Axes of the slice: x: 4, y: 4, z: 8, core: 2. Of those that a mesh axis runs over, the one named last changes fastest.
Arguments:
- integrals: bfloat16 [1024, 1024, 1024], P(('quartet', 'pert')), may hold values from -0.1875 to 0.1875
- quartets: int32 [1024, 4], P(('quartet', 'pert')), may hold values from 0 to 63, as said below
- density: bfloat16 [131072, 2048], P(('quartet', 'pert')), may hold values from -6 to 6
- orbitals: bfloat16 [2048, 256], replicated, may hold values from -0.125 to 0.125
Outputs:
- response: float32 [131072, 256], P(('quartet', 'pert'))
The draws below stay inside these ranges and needn't reach their ends.
Inputs may be any that keep to these rules, and one draw needn't show every extreme that they name: `quartets`: rows 4 m to 4 m + 3 are the quartet blocks of one device. Within such a group the first blocks lie in four different quarters of the 64 shell blocks (quarter = block // 16), and so do the second blocks and the third blocks.
All inputs are finite; a program needn't handle non-finite values.
Results may differ from the reference program's by a relative error of at most 0.0029.
Values may be sent and summed in bfloat16 or wider, within the bound.
A program may use at most 256 MiB of HBM per device.

```python
import jax
import jax.numpy as jnp
from jax import lax

N = 2048
O = 256
P_SIZE = 64
S = 32
NB = 64
QUARTETS = 1024


def draw_quartets(key, part):
    key = jax.random.fold_in(key, 11)
    groups = QUARTETS // 4
    quarter_span = NB // 4

    def one_group(group_key):
        group_keys = jax.random.split(group_key, 7)
        roles = []
        for role_index in range(3):
            quarters = jax.random.permutation(group_keys[role_index], 4)
            offsets = jax.random.randint(group_keys[3 + role_index], (4,), 0, quarter_span)
            roles.append(quarters * quarter_span + offsets)
        roles.append(jax.random.randint(group_keys[6], (4,), 0, NB))
        return jnp.stack(roles, axis=-1).astype(jnp.int32)
    return jax.vmap(one_group)(jax.random.split(key, groups)).reshape(QUARTETS, 4)


def shard_levels(rng, dims, cuts, low, top_value):
    level, own = 1.0, jax.random.fold_in(rng, 6)
    for position, shards_of in cuts:
        draws = jnp.exp(jax.random.uniform(jax.random.fold_in(own, position), (shards_of,), jnp.float32, low / len(cuts), top_value / len(cuts)))
        level = level * jnp.repeat(draws, dims[position] // shards_of).reshape([-1 if axis == position else 1 for axis in range(len(dims))])
    return level


def noise(key, extent, spread, reach, cuts=(), dtype=jnp.bfloat16):
    level = shard_levels(key, extent, cuts, -0.22, 0.18) if cuts else 1.0
    array = jax.random.normal(key, extent, jnp.float32) * spread * level
    return jnp.minimum(jnp.maximum(array, -reach), reach).astype(dtype)


def setup_inputs(seed: int = 0) -> dict:
    key_of = jax.random.split(jax.random.key(seed), 5)
    return {
        "integrals": noise(key_of[0], (QUARTETS, S * S, S * S), (S * S) ** -0.5, 0.1875, ((0, 256),)),
        "quartets": draw_quartets(jax.random.fold_in(key_of[4], 71), 0),
        "density": noise(key_of[2], (P_SIZE * N, N), 1.0, 6.0, ((0, 256),)),
        "orbitals": noise(key_of[3], (N, O), N ** -0.5, 0.125),
    }


def digest(integral, gathered):
    pert_count = gathered.shape[1]
    integral_four = integral.reshape(S, S, S, S)
    coulomb_bra = jnp.einsum("xc,bc->xb", gathered[0], integral, preferred_element_type=jnp.float32)
    coulomb_ket = jnp.einsum("xb,bc->xc", gathered[1], integral, preferred_element_type=jnp.float32)
    exchange_ik = jnp.einsum("xrt,prst->xps", gathered[2].reshape(pert_count, S, S), integral_four, preferred_element_type=jnp.float32)
    exchange_il = jnp.einsum("xrs,prst->xpt", gathered[3].reshape(pert_count, S, S), integral_four, preferred_element_type=jnp.float32)
    exchange_jk = jnp.einsum("xpt,prst->xrs", gathered[4].reshape(pert_count, S, S), integral_four, preferred_element_type=jnp.float32)
    exchange_jl = jnp.einsum("xps,prst->xrt", gathered[5].reshape(pert_count, S, S), integral_four, preferred_element_type=jnp.float32)
    flat = (pert_count, S * S)
    return jnp.stack([coulomb_bra, coulomb_ket, -0.5 * exchange_ik.reshape(flat), -0.5 * exchange_il.reshape(flat),
                      -0.5 * exchange_jk.reshape(flat), -0.5 * exchange_jl.reshape(flat)])


def reference(integrals, quartets, density, orbitals):
    density_tiles = density.reshape(P_SIZE, NB, S, NB, S).transpose(1, 3, 0, 2, 4).reshape(NB * NB, P_SIZE, S * S)

    def absorb(fock_sum, payload):
        integral, blocks = payload
        bra_one, bra_two, ket_one, ket_two = blocks[0], blocks[1], blocks[2], blocks[3]
        needed = jnp.stack([ket_one * NB + ket_two, bra_one * NB + bra_two, bra_two * NB + ket_two,
                            bra_two * NB + ket_one, bra_one * NB + ket_two, bra_one * NB + ket_one]).astype(jnp.int32)
        gathered = density_tiles[needed].astype(jnp.float32)
        pieces = digest(integral.astype(jnp.float32), gathered)
        output_ids = jnp.stack([bra_one * NB + bra_two, ket_one * NB + ket_two, bra_one * NB + ket_one,
                                bra_one * NB + ket_two, bra_two * NB + ket_one, bra_two * NB + ket_two]).astype(jnp.int32)
        return fock_sum.at[output_ids].add(pieces), None

    fock_start = jnp.zeros((NB * NB, P_SIZE, S * S), jnp.float32)
    fock_sum, _ = lax.scan(absorb, fock_start, (integrals, quartets))
    fock_rounded = lax.optimization_barrier(fock_sum.astype(jnp.bfloat16)).astype(jnp.float32)
    result = jnp.einsum("abxpq,bqo->xapo", fock_rounded.reshape(NB, NB, P_SIZE, S, S),
                        orbitals.astype(jnp.float32).reshape(NB, S, O), preferred_element_type=jnp.float32)
    return result.reshape(P_SIZE * N, O)
```

```python
import functools

import jax
import jax.numpy as jnp
from jax import lax
from jax.experimental import pallas as pl
from jax.experimental.pallas import tpu as pltpu
from jax.sharding import PartitionSpec as P

P_SIZE = 64
S = 32
NB = 64
QUARTERS = 4
SPAN = NB // QUARTERS
GROUP = 4
SLOTS = 6
LANES = 128
SUB = 8
AREA = S * S
CHUNK = SLOTS * SUB
SCALE = 32.0

f32 = jnp.float32
bf16 = jnp.bfloat16
f16 = jnp.float16


def swap_groups(parts):
    lane = lax.broadcasted_iota(jnp.int32, parts[0].shape, len(parts[0].shape) - 1)
    axis = len(parts[0].shape) - 1
    low_half = lane < 64
    even = (lane // 32) % 2 == 0
    v0, v1, v2, v3 = parts
    u0 = jnp.where(low_half, v0, pltpu.roll(v2, 64, axis))
    u2 = jnp.where(low_half, pltpu.roll(v0, 64, axis), v2)
    u1 = jnp.where(low_half, v1, pltpu.roll(v3, 64, axis))
    u3 = jnp.where(low_half, pltpu.roll(v1, 64, axis), v3)
    w0 = jnp.where(even, u0, pltpu.roll(u1, 32, axis))
    w1 = jnp.where(even, pltpu.roll(u0, 96, axis), u1)
    w2 = jnp.where(even, u2, pltpu.roll(u3, 32, axis))
    w3 = jnp.where(even, pltpu.roll(u2, 96, axis), u3)
    return [w0, w1, w2, w3]


def tiles_kernel(dens_ref, tiles_ref, turned_ref, rows_ref, flip_ref):
    rows_ref[...] = dens_ref[...].astype(f32)
    for a in range(SPAN):
        parts = [rows_ref[pl.ds(S * a + s, SUB, stride=4), :] for s in range(4)]
        for b, tile in enumerate(swap_groups(parts)):
            tiles_ref[b * SPAN + a] = tile
    for big in range(4):
        flip_ref[...] = rows_ref[LANES * big : LANES * (big + 1), :].T
        for b in range(4):
            parts = [flip_ref[pl.ds(S * b + t, SUB, stride=4), :] for t in range(4)]
            for a, tile in enumerate(swap_groups(parts)):
                turned_ref[b * SPAN + 4 * big + a] = tile


def cut_tiles(density):
    rows, columns = density.shape
    steps = columns // LANES
    tiles = jax.ShapeDtypeStruct((NB * SPAN, SUB, LANES), f32)
    block = pl.BlockSpec((4 * SPAN, SUB, LANES), lambda i: (i, 0, 0))
    return pl.pallas_call(
        tiles_kernel,
        grid=(steps,),
        in_specs=[pl.BlockSpec((rows, LANES), lambda i: (0, i))],
        out_specs=[block, block],
        out_shape=[tiles, tiles],
        scratch_shapes=[pltpu.VMEM((rows, LANES), f32), pltpu.VMEM((LANES, LANES), f32)],
        name="cut_tiles",
    )(density)


def pick_kernel(index_ref, tiles_ref, turned_ref, out_ref):
    per_step = out_ref.shape[0]
    first = pl.program_id(0) * per_step

    def one(n, carry):
        e = first + n
        at = [index_ref[r, e] for r in range(SLOTS)]
        pairs = (
            (tiles_ref[at[0]], turned_ref[at[1]]),
            (tiles_ref[at[2]], turned_ref[at[3]]),
            (tiles_ref[at[4]], tiles_ref[at[5]]),
        )
        for r, pair in enumerate(pairs):
            out_ref[n, 16 * r : 16 * (r + 1), :] = jnp.concatenate(pair, axis=0).astype(bf16)
        return carry

    lax.fori_loop(0, per_step, one, 0, unroll=4)


def pick_tiles(index, tiles, turned):
    devices = index.shape[1]
    per_step = 32
    whole = pl.BlockSpec(tiles.shape, lambda i, index: (0, 0, 0))
    return pl.pallas_call(
        pick_kernel,
        grid_spec=pltpu.PrefetchScalarGridSpec(
            num_scalar_prefetch=1,
            grid=(devices // per_step,),
            in_specs=[whole, whole],
            out_specs=pl.BlockSpec((per_step, CHUNK, LANES), lambda i, index: (i, 0, 0)),
        ),
        out_shape=jax.ShapeDtypeStruct((devices, CHUNK, LANES), bf16),
        compiler_params=pltpu.CompilerParams(vmem_limit_bytes=40 << 20),
        name="pick_tiles",
    )(index, tiles, turned)


def pairings_kernel(g_ref, ps_ref, sp_ref, rows_ref):
    rows_ref[...] = g_ref[0].astype(f32)
    for big in range(8):
        lanes = slice(LANES * big, LANES * (big + 1))
        parts = [g_ref[0, S * (4 * big + p) : S * (4 * big + p + 1), :] for p in range(4)]
        for s, block in enumerate(swap_groups(parts)):
            sp_ref[0, S * s : S * (s + 1), lanes] = block
        parts = [rows_ref[pl.ds(4 * big + r, S, stride=S), :].astype(bf16) for r in range(4)]
        for s, block in enumerate(swap_groups(parts)):
            ps_ref[0, S * s : S * (s + 1), lanes] = block


def pairings(integrals):
    count = integrals.shape[0]
    shape = jax.ShapeDtypeStruct(integrals.shape, bf16)
    block = pl.BlockSpec((1, LANES, AREA), lambda m, c: (m, c, 0))
    return pl.pallas_call(
        pairings_kernel,
        grid=(count, AREA // LANES),
        in_specs=[pl.BlockSpec((1, AREA, LANES), lambda m, c: (m, 0, c))],
        out_specs=[block, block],
        out_shape=[shape, shape],
        scratch_shapes=[pltpu.VMEM((AREA, LANES), f32)],
        cost_estimate=pl.CostEstimate(
            flops=40_000_000_000, bytes_accessed=3 * 2 * count * AREA * AREA, transcendentals=0
        ),
        name="pairings",
    )(integrals)


def digest_kernel(quarter_ref, recv_ref, g_ref, ps_ref, sp_ref, out_ref, rows_ref):
    m = pl.program_id(0)

    @pl.when(m == 0)
    def _():
        def widen(x, carry):
            at = pl.multiple_of(x * QUARTERS * CHUNK, QUARTERS * CHUNK)
            rows_ref[pl.ds(at, QUARTERS * CHUNK), :] = recv_ref[
                pl.ds(at, QUARTERS * CHUNK), :
            ].astype(f32)
            return carry

        lax.fori_loop(0, P_SIZE, widen, 0)

    stride = QUARTERS * CHUNK
    q_i, q_j, q_k = (quarter_ref[3 * m + role] for role in range(3))

    def fetch(quarter, slot):
        first = quarter * CHUNK + slot * SUB
        return jnp.concatenate(
            [
                rows_ref[pl.ds(first + c, P_SIZE, stride=stride), :].astype(bf16)
                for c in range(SUB)
            ],
            axis=1,
        )

    def put(quarter, slot, value):
        first = quarter * CHUNK + slot * SUB
        for c in range(SUB):
            out_ref[pl.ds(first + c, P_SIZE, stride=stride), :] = value[
                :, LANES * c : LANES * (c + 1)
            ]

    def times(left, right):
        return jnp.dot(left, right, preferred_element_type=f32)

    def times_turned(left, right):
        return lax.dot_general(
            left, right, (((1,), (1,)), ((), ())), preferred_element_type=f32
        )

    g, ps, sp = g_ref[0], ps_ref[0], sp_ref[0]
    half = -0.5 * SCALE
    put(q_i, 0, SCALE * times_turned(fetch(q_k, 4), g))
    put(q_k, 4, SCALE * times(fetch(q_i, 0), g))
    put(q_i, 1, half * times_turned(fetch(q_j, 2), ps))
    put(q_j, 2, half * times(fetch(q_i, 1), ps))
    put(q_i, 5, half * times(fetch(q_j, 3), sp))
    put(q_j, 3, half * times_turned(fetch(q_i, 5), sp))


def digest(quarters, received, integrals, ps, sp):
    count = integrals.shape[0]
    rows = received.shape[0]
    square = pl.BlockSpec((1, AREA, AREA), lambda m, q: (m, 0, 0))
    whole = pl.BlockSpec((rows, LANES), lambda m, q: (0, 0))
    return pl.pallas_call(
        digest_kernel,
        grid_spec=pltpu.PrefetchScalarGridSpec(
            num_scalar_prefetch=1,
            grid=(count,),
            in_specs=[whole, square, square, square],
            out_specs=whole,
            scratch_shapes=[pltpu.VMEM((rows, LANES), f32)],
        ),
        out_shape=jax.ShapeDtypeStruct((rows, LANES), f32),
        compiler_params=pltpu.CompilerParams(vmem_limit_bytes=56 << 20),
        name="digest",
    )(quarters, received, integrals, ps, sp)


def finish_kernel(
    index_ref, recv_ref, orb_ref, out_ref, tiles_ref, turned_ref, rows_ref, flip_ref, fock_ref
):
    step = pl.program_id(0)
    per_step = recv_ref.shape[0]

    @pl.when(step == 0)
    def _():
        tiles_ref[...] = jnp.zeros_like(tiles_ref)
        turned_ref[...] = jnp.zeros_like(turned_ref)

    def one(n, carry):
        e = step * per_step + n
        for slot, target in enumerate(
            (tiles_ref, turned_ref, tiles_ref, turned_ref, tiles_ref, tiles_ref)
        ):
            at = index_ref[slot, e]
            target[at] = target[at] + recv_ref[n, SUB * slot : SUB * (slot + 1), :]
        return carry

    lax.fori_loop(0, per_step, one, 0, unroll=4)

    @pl.when(step == pl.num_programs(0) - 1)
    def _():
        def column(c, carry):
            base = c * 4 * SPAN
            for a in range(SPAN):
                parts = [tiles_ref[base + b * SPAN + a] for b in range(4)]
                for s, block in enumerate(swap_groups(parts)):
                    rows_ref[pl.ds(S * a + s, SUB, stride=4), :] = block
            for big in range(4):
                for b in range(4):
                    parts = [turned_ref[base + b * SPAN + 4 * big + a] for a in range(4)]
                    for t, block in enumerate(swap_groups(parts)):
                        flip_ref[pl.ds(S * b + t, SUB, stride=4), :] = block
                rows = slice(LANES * big, LANES * (big + 1))
                total = rows_ref[rows, :] + flip_ref[...].T
                fock_ref[rows, pl.ds(pl.multiple_of(c * LANES, LANES), LANES)] = (
                    total * (1.0 / SCALE)
                ).astype(bf16)
            return carry

        lax.fori_loop(0, NB // 4, column, 0)
        out_ref[...] = jnp.dot(fock_ref[...], orb_ref[...], preferred_element_type=f32)


def finish(index, arrived, orbitals, rows):
    devices = index.shape[1]
    per_step = 32
    basis, occupied = orbitals.shape
    return pl.pallas_call(
        finish_kernel,
        grid_spec=pltpu.PrefetchScalarGridSpec(
            num_scalar_prefetch=1,
            grid=(devices // per_step,),
            in_specs=[
                pl.BlockSpec((per_step, CHUNK, LANES), lambda i, index: (i, 0, 0)),
                pl.BlockSpec((basis, occupied), lambda i, index: (0, 0)),
            ],
            out_specs=pl.BlockSpec((rows, occupied), lambda i, index: (0, 0)),
            scratch_shapes=[
                pltpu.VMEM((NB * SPAN, SUB, LANES), f32),
                pltpu.VMEM((NB * SPAN, SUB, LANES), f32),
                pltpu.VMEM((rows, LANES), f32),
                pltpu.VMEM((LANES, LANES), f32),
                pltpu.VMEM((rows, basis), bf16),
            ],
        ),
        out_shape=jax.ShapeDtypeStruct((rows, occupied), f32),
        compiler_params=pltpu.CompilerParams(vmem_limit_bytes=40 << 20),
        name="finish",
    )(index, arrived, orbitals)


def tile_index(lists, quarter):
    i, j, k, l = (lists[:, :, role] for role in range(4))
    low = quarter * SPAN
    of_i = i // SPAN == quarter
    of_j = j // SPAN == quarter
    of_k = k // SPAN == quarter

    def pick(mask, value):
        return jnp.sum(jnp.where(mask, value, 0), axis=0)

    return jnp.stack(
        [
            pick(of_i, j * SPAN + i - low),
            pick(of_i, k * SPAN + i - low),
            pick(of_j, l * SPAN + j - low),
            pick(of_j, k * SPAN + j - low),
            pick(of_k, l * SPAN + k - low),
            pick(of_i, l * SPAN + i - low),
        ]
    )


def per_device(integrals, quartets, density, orbitals):
    axes = ("quartet", "pert")
    devices = lax.axis_size("quartet") * lax.axis_size("pert")
    myself = lax.axis_index("quartet") * lax.axis_size("pert") + lax.axis_index("pert")
    quarter = myself % QUARTERS

    flat = jnp.pad(quartets.reshape(1, GROUP * 4), ((0, 0), (0, LANES - GROUP * 4)))
    gathered = lax.all_gather(jnp.broadcast_to(flat, (SUB, LANES)), axes, axis=0, tiled=True)
    tiles, turned = cut_tiles(density)
    lists = gathered.reshape(devices, SUB, LANES)[:, 0, : GROUP * 4].T.reshape(GROUP, 4, devices)
    index = tile_index(lists.transpose(0, 2, 1), quarter)

    outgoing = pick_tiles(index, tiles, turned)
    received = lax.all_to_all(outgoing, axes, 0, 0, tiled=True)
    ps, sp = pairings(integrals)
    quarters = (quartets[:, :3] // SPAN).reshape(-1)
    terms = digest(quarters, received.reshape(-1, LANES), integrals, ps, sp)
    leaving = terms.astype(f16).reshape(devices, CHUNK, LANES)
    landed = lax.all_to_all(leaving, axes, 0, 0, tiled=True)
    return finish(index, landed.astype(f32), orbitals, density.shape[0])


def solution(mesh):
    placed = (
        P(("quartet", "pert"), None, None),
        P(("quartet", "pert"), None),
        P(("quartet", "pert"), None),
        P(),
    )
    return jax.shard_map(
        per_device,
        mesh=mesh,
        in_specs=placed,
        out_specs=P(("quartet", "pert"), None),
        check_vma=False,
    )
```

```python
import jax
import jax.numpy as jnp
import numpy as np
from jax import lax
from jax.experimental import pallas as pl
from jax.experimental.pallas import tpu as pltpu
from jax.sharding import PartitionSpec as P

P_SIZE = 64
S = 32
NB = 64
QUARTERS = 4
SPAN = NB // QUARTERS
GROUP = 4
SLOTS = 6
LANES = 128
SUB = 8
AREA = S * S
CHUNK = SLOTS * SUB
SCALE = 32.0

f32 = jnp.float32
bf16 = jnp.bfloat16
f16 = jnp.float16


def group_swap():
    eye = np.eye(4 * LANES, dtype=np.float32)
    return jnp.asarray(eye.reshape(4, 4, S, 4 * LANES).transpose(1, 0, 2, 3).reshape(eye.shape), bf16)


def times(left, right):
    return jnp.dot(left, right, preferred_element_type=f32)


def times_turned(left, right):
    return lax.dot_general(left, right, (((1,), (1,)), ((), ())), preferred_element_type=f32)


def tiles_kernel(dens_ref, swap_ref, tiles_ref, rows_ref):
    width = dens_ref.shape[1] // LANES
    parts = []
    for n in range(width):
        rows_ref[n] = dens_ref[:, LANES * n : LANES * (n + 1)].astype(f32)
        parts.append(
            jnp.concatenate(
                [rows_ref[n, pl.ds(s, LANES, stride=4), :].astype(bf16) for s in range(4)], axis=1
            )
        )
    out = times(jnp.concatenate(parts, axis=0), swap_ref[...])
    for n in range(width):
        for b in range(4):
            tiles_ref[(4 * n + b) * SPAN : (4 * n + b + 1) * SPAN] = out[
                LANES * n : LANES * (n + 1), LANES * b : LANES * (b + 1)
            ].reshape(SPAN, SUB, LANES)


def cut_tiles(density, swap):
    rows, columns = density.shape
    width = 2
    return pl.pallas_call(
        tiles_kernel,
        grid=(columns // (width * LANES),),
        in_specs=[
            pl.BlockSpec((rows, width * LANES), lambda i: (0, i)),
            pl.BlockSpec(swap.shape, lambda i: (0, 0)),
        ],
        out_specs=pl.BlockSpec((width * 4 * SPAN, SUB, LANES), lambda i: (i, 0, 0)),
        out_shape=jax.ShapeDtypeStruct((NB * SPAN, SUB, LANES), f32),
        scratch_shapes=[pltpu.VMEM((width, rows, LANES), f32)],
        cost_estimate=pl.CostEstimate(
            flops=4_000_000_000, bytes_accessed=6 * rows * columns, transcendentals=0
        ),
        name="cut_tiles",
    )(density, swap)


def pick_kernel(index_ref, tiles_ref, out_ref):
    per_step = out_ref.shape[0]
    first = pl.program_id(0) * per_step

    def one(n, carry):
        for pair in range(SLOTS // 2):
            halves = [tiles_ref[index_ref[2 * pair + h, first + n]] for h in range(2)]
            out_ref[n, 16 * pair : 16 * (pair + 1), :] = jnp.concatenate(halves, axis=0).astype(
                bf16
            )
        return carry

    lax.fori_loop(0, per_step, one, 0, unroll=8)


def pick_tiles(index, tiles):
    devices = index.shape[1]
    per_step = 64
    return pl.pallas_call(
        pick_kernel,
        grid_spec=pltpu.PrefetchScalarGridSpec(
            num_scalar_prefetch=1,
            grid=(devices // per_step,),
            in_specs=[pl.BlockSpec(memory_space=pltpu.VMEM)],
            out_specs=pl.BlockSpec((per_step, CHUNK, LANES), lambda i, index: (i, 0, 0)),
        ),
        out_shape=jax.ShapeDtypeStruct((devices, CHUNK, LANES), bf16),
        compiler_params=pltpu.CompilerParams(vmem_limit_bytes=58 << 20),
        name="pick_tiles",
    )(index, tiles)


def pairings_kernel(g_ref, swap_ref, ps_ref, rs_ref, rows_ref, ps_rows, rs_rows):
    step = pl.program_id(1)
    rows_ref[...] = g_ref[0].astype(f32)
    swap = swap_ref[...]

    def spread(parts, target):
        out = times(jnp.concatenate(parts, axis=1), swap)
        for big in range(8):
            for s in range(4):
                target[big, pl.ds(4 * step + s, S, stride=S), :] = out[
                    S * big : S * (big + 1), LANES * s : LANES * (s + 1)
                ]

    spread(
        [
            jnp.concatenate(
                [rows_ref[pl.ds(4 * big + r, S, stride=S), :] for big in range(8)], axis=0
            ).astype(bf16)
            for r in range(4)
        ],
        ps_rows,
    )
    spread(
        [
            jnp.concatenate(
                [g_ref[0, S * (4 * big + p) : S * (4 * big + p + 1), :] for big in range(8)],
                axis=0,
            )
            for p in range(4)
        ],
        rs_rows,
    )

    @pl.when(step == pl.num_programs(1) - 1)
    def _():
        for big in range(8):
            lanes = slice(LANES * big, LANES * (big + 1))
            ps_ref[0, :, lanes] = ps_rows[big].astype(bf16)
            rs_ref[0, :, lanes] = rs_rows[big].astype(bf16)


def pairings(integrals, swap):
    count = integrals.shape[0]
    shape = jax.ShapeDtypeStruct(integrals.shape, bf16)
    block = pl.BlockSpec((1, AREA, AREA), lambda m, c: (m, 0, 0))
    return pl.pallas_call(
        pairings_kernel,
        grid=(count, AREA // LANES),
        in_specs=[
            pl.BlockSpec((1, AREA, LANES), lambda m, c: (m, 0, c)),
            pl.BlockSpec(swap.shape, lambda m, c: (0, 0)),
        ],
        out_specs=[block, block],
        out_shape=[shape, shape],
        scratch_shapes=[pltpu.VMEM((AREA, LANES), f32)]
        + [pltpu.VMEM((AREA // LANES, AREA, LANES), f32)] * 2,
        compiler_params=pltpu.CompilerParams(vmem_limit_bytes=56 << 20),
        cost_estimate=pl.CostEstimate(
            flops=40_000_000_000, bytes_accessed=3 * 2 * count * AREA * AREA, transcendentals=0
        ),
        name="pairings",
    )(integrals, swap)


def digest_kernel(quarter_ref, recv_ref, g_ref, ps_ref, rs_ref, out_ref, rows_ref):
    m = pl.program_id(0)

    @pl.when(m == 0)
    def _():
        def widen(x, carry):
            at = pl.multiple_of(x * QUARTERS * CHUNK, QUARTERS * CHUNK)
            rows_ref[pl.ds(at, QUARTERS * CHUNK), :] = recv_ref[
                pl.ds(at, QUARTERS * CHUNK), :
            ].astype(f32)
            return carry

        lax.fori_loop(0, P_SIZE, widen, 0)

    stride = QUARTERS * CHUNK
    q_i, q_j, q_k = (quarter_ref[3 * m + role] for role in range(3))

    def fetch(quarter, slot):
        first = quarter * CHUNK + slot * SUB
        return jnp.concatenate(
            [
                rows_ref[pl.ds(first + c, P_SIZE, stride=stride), :].astype(bf16)
                for c in range(SUB)
            ],
            axis=1,
        )

    def put(quarter, slot, value):
        first = quarter * CHUNK + slot * SUB
        for c in range(SUB):
            out_ref[pl.ds(first + c, P_SIZE, stride=stride), :] = value[
                :, LANES * c : LANES * (c + 1)
            ]

    g, ps, rs = g_ref[0], ps_ref[0], rs_ref[0]
    half = -0.5 * SCALE
    put(q_i, 0, SCALE * times_turned(fetch(q_k, 4), g))
    put(q_k, 4, SCALE * times(fetch(q_i, 0), g))
    put(q_i, 1, half * times_turned(fetch(q_j, 2), ps))
    put(q_j, 2, half * times(fetch(q_i, 1), ps))
    put(q_i, 5, half * times(fetch(q_j, 3), rs))
    put(q_j, 3, half * times_turned(fetch(q_i, 5), rs))


def digest(quarters, received, integrals, ps, rs):
    count = integrals.shape[0]
    rows = received.shape[0]
    square = pl.BlockSpec((1, AREA, AREA), lambda m, q: (m, 0, 0))
    whole = pl.BlockSpec(memory_space=pltpu.VMEM)
    return pl.pallas_call(
        digest_kernel,
        grid_spec=pltpu.PrefetchScalarGridSpec(
            num_scalar_prefetch=1,
            grid=(count,),
            in_specs=[whole, square, square, square],
            out_specs=whole,
            scratch_shapes=[pltpu.VMEM((rows, LANES), f32)],
        ),
        out_shape=jax.ShapeDtypeStruct((rows, LANES), f32),
        compiler_params=pltpu.CompilerParams(vmem_limit_bytes=44 << 20),
        name="digest",
    )(quarters, received, integrals, ps, rs)


def finish_kernel(index_ref, recv_ref, orb_ref, swap_ref, out_ref, sums_ref, rows_ref, fock_ref):
    chains = sums_ref.shape[0]

    def clear(n, carry):
        sums_ref[:, pl.ds(SPAN * n, SPAN)] = jnp.zeros((chains, SPAN, SUB, LANES), f32)
        return carry

    lax.fori_loop(0, NB, clear, 0)

    def one(e, carry):
        for turn in range(SLOTS // chains):
            for chain in range(chains):
                slot = turn * chains + chain
                at = index_ref[slot, e]
                sums_ref[chain, at] = (
                    sums_ref[chain, at] + recv_ref[e, SUB * slot : SUB * (slot + 1), :]
                )
        return carry

    lax.fori_loop(0, recv_ref.shape[0], one, 0, unroll=4)

    def column(c, carry):
        parts = []
        for b in range(4):
            tiles = pl.ds((4 * c + b) * SPAN, SPAN)
            total = sums_ref[0, tiles]
            for chain in range(1, chains):
                total = total + sums_ref[chain, tiles]
            parts.append((total * (1.0 / SCALE)).astype(bf16).reshape(SPAN * SUB, LANES))
        out = times(jnp.concatenate(parts, axis=1), swap_ref[...])
        for s in range(4):
            rows_ref[pl.ds(s, LANES, stride=4), :] = out[:, LANES * s : LANES * (s + 1)]
        fock_ref[:, pl.ds(pl.multiple_of(c * LANES, LANES), LANES)] = rows_ref[...].astype(bf16)
        return carry

    lax.fori_loop(0, NB // 4, column, 0, unroll=2)
    out_ref[...] = times(fock_ref[...], orb_ref[...])


def finish(index, arrived, orbitals, swap, rows):
    basis, occupied = orbitals.shape
    chains = 3
    whole = pl.BlockSpec(memory_space=pltpu.VMEM)
    return pl.pallas_call(
        finish_kernel,
        in_specs=[pl.BlockSpec(memory_space=pltpu.SMEM), whole, whole, whole],
        out_specs=whole,
        scratch_shapes=[
            pltpu.VMEM((chains, NB * SPAN, SUB, LANES), f32),
            pltpu.VMEM((rows, LANES), f32),
            pltpu.VMEM((rows, basis), bf16),
        ],
        out_shape=jax.ShapeDtypeStruct((rows, occupied), f32),
        compiler_params=pltpu.CompilerParams(vmem_limit_bytes=32 << 20),
        name="finish",
    )(index, arrived, orbitals, swap)


def tile_index(lists, quarter):
    i, j, k, l = (lists[:, :, role] for role in range(4))
    low = quarter * SPAN
    of_i = i // SPAN == quarter
    of_j = j // SPAN == quarter
    of_k = k // SPAN == quarter

    def pick(mask, value):
        return jnp.sum(jnp.where(mask, value, 0), axis=0)

    return jnp.stack(
        [
            pick(of_i, j * SPAN + i - low),
            pick(of_i, k * SPAN + i - low),
            pick(of_j, l * SPAN + j - low),
            pick(of_j, k * SPAN + j - low),
            pick(of_k, l * SPAN + k - low),
            pick(of_i, l * SPAN + i - low),
        ]
    )


def per_device(integrals, quartets, density, orbitals):
    axes = ("quartet", "pert")
    devices = lax.axis_size("quartet") * lax.axis_size("pert")
    myself = lax.axis_index("quartet") * lax.axis_size("pert") + lax.axis_index("pert")
    quarter = myself % QUARTERS

    swap = group_swap()
    flat = jnp.pad(quartets.reshape(1, 1, GROUP * 4), ((0, 0), (0, 0), (0, LANES - GROUP * 4)))
    lists = lax.all_to_all(
        jnp.broadcast_to(flat, (devices, 1, LANES)), axes, split_axis=0, concat_axis=0, tiled=True
    )
    tiles = cut_tiles(density, swap)
    lists = lists.reshape(devices, LANES).T[: GROUP * 4].reshape(GROUP, 4, devices)
    index = tile_index(lists.transpose(0, 2, 1), quarter)

    outgoing = pick_tiles(index, tiles)
    received = lax.all_to_all(outgoing, axes, 0, 0, tiled=True)
    ps, rs = pairings(integrals, swap)
    quarters = (quartets[:, :3] // SPAN).reshape(-1)
    terms = digest(quarters, received.reshape(-1, LANES), integrals, ps, rs)
    leaving = terms.astype(f16).reshape(devices, CHUNK, LANES)
    landed = lax.all_to_all(leaving, axes, 0, 0, tiled=True)
    return finish(index, landed.astype(f32), orbitals, swap, density.shape[0])


def solution(mesh):
    placed = (
        P(("quartet", "pert"), None, None),
        P(("quartet", "pert"), None),
        P(("quartet", "pert"), None),
        P(),
    )
    return jax.shard_map(
        per_device,
        mesh=mesh,
        in_specs=placed,
        out_specs=P(("quartet", "pert"), None),
        check_vma=False,
    )
```

```python
import jax
import jax.numpy as jnp
import numpy as np
from jax import lax
from jax.experimental import pallas as pl
from jax.experimental.pallas import tpu as pltpu
from jax.sharding import PartitionSpec as P

P_SIZE = 64
S = 32
NB = 64
QUARTERS = 4
SPAN = NB // QUARTERS
GROUP = 4
SLOTS = 6
LANES = 128
SUB = 8
AREA = S * S
CHUNK = SLOTS * SUB
SCALE = 32.0

MESH = pl.DeviceIdType.MESH
SPREAD_VMEM = 57 << 20
PICK_VMEM = 58 << 20
PAIRINGS_VMEM = 56 << 20
DIGEST_VMEM = 44 << 20

f32 = jnp.float32
bf16 = jnp.bfloat16
f16 = jnp.float16


def group_swap():
    eye = np.eye(4 * LANES, dtype=np.float32)
    return jnp.asarray(eye.reshape(4, 4, S, 4 * LANES).transpose(1, 0, 2, 3).reshape(eye.shape), bf16)


def times(left, right):
    return jnp.dot(left, right, preferred_element_type=f32)


def times_turned(left, right):
    return lax.dot_general(left, right, (((1,), (1,)), ((), ())), preferred_element_type=f32)


def spread_kernel(
    list_ref,
    dens_from,
    swap_from,
    lists_ref,
    tiles_to,
    tiles_ref,
    rows_ref,
    dens_ref,
    swap_ref,
    send_sem,
    recv_sem,
    own_sem,
    store_sem,
):
    chip, core = lax.axis_index("quartet"), lax.axis_index("pert")
    x, y, z = chip % 4, (chip // 4) % 4, chip // 16
    steps = (
        (2 * chip + core, 1, [(chip, (core + 1) % 2)]),
        (2 * chip, 2, [(chip - x + (x + n) % 4, core) for n in range(1, 4)]),
        (8 * (chip // 4), 8, [(chip - 4 * y + 4 * ((y + n) % 4), core) for n in range(1, 4)]),
        (32 * z, 32, [(chip - 16 * z + 16 * ((z + n) % 8), core) for n in range(1, 8)]),
    )
    barrier = pltpu.get_barrier_semaphore()
    for _, _, partners in steps:
        for partner in partners:
            pl.semaphore_signal(barrier, inc=1, device_id=partner, device_id_type=MESH)
    own = pltpu.make_async_copy(list_ref, lists_ref.at[pl.ds(2 * chip + core, 1)], own_sem.at[0])
    own.start()
    fetches = (
        pltpu.make_async_copy(dens_from, dens_ref, own_sem.at[1]),
        pltpu.make_async_copy(swap_from, swap_ref, own_sem.at[2]),
    )
    for fetch in fetches:
        fetch.start()

    wide = rows_ref.shape[0]

    def cut(n):
        parts = []
        for w in range(wide):
            columns = slice(LANES * (wide * n + w), LANES * (wide * n + w + 1))
            rows_ref[w] = dens_ref[:, columns].astype(f32)
            parts.append(
                jnp.concatenate(
                    [rows_ref[w, pl.ds(s, LANES, stride=4), :].astype(bf16) for s in range(4)],
                    axis=1,
                )
            )
        out = times(jnp.concatenate(parts, axis=0), swap_ref[...])
        for w in range(wide):
            for b in range(4):
                first = (4 * (wide * n + w) + b) * SPAN
                tiles_ref[first : first + SPAN] = out[
                    LANES * w : LANES * (w + 1), LANES * b : LANES * (b + 1)
                ].reshape(SPAN, SUB, LANES)

    own.wait()
    pl.semaphore_wait(barrier, sum(len(partners) for _, _, partners in steps))
    stores = []
    for n, (first, count, partners) in enumerate(steps):
        block = lists_ref.at[pl.ds(first, count)]
        for partner in partners:
            pltpu.make_async_remote_copy(
                src_ref=block,
                dst_ref=block,
                send_sem=send_sem.at[n],
                recv_sem=recv_sem.at[n],
                device_id=partner,
                device_id_type=MESH,
            ).start()
        if n == 0:
            for fetch in fetches:
                fetch.wait()
        cut(n)
        part = pl.ds(n * wide * 4 * SPAN, wide * 4 * SPAN)
        stores.append(
            pltpu.make_async_copy(tiles_ref.at[part], tiles_to.at[part], store_sem.at[n])
        )
        stores[n].start()
        bytes_in = lists_ref.at[pl.ds(0, count * len(partners))]
        pltpu.make_async_copy(bytes_in, bytes_in, recv_sem.at[n]).wait()
    for n, (_, count, partners) in enumerate(steps):
        bytes_out = lists_ref.at[pl.ds(0, count * len(partners))]
        pltpu.make_async_copy(bytes_out, bytes_out, send_sem.at[n]).wait()
        stores[n].wait()


def spread_and_cut(own_list, density, swap, devices):
    rows, columns = density.shape
    wide = columns // LANES // 4
    whole = pl.BlockSpec(memory_space=pltpu.VMEM)
    far = pl.BlockSpec(memory_space=pl.ANY)
    return pl.pallas_call(
        spread_kernel,
        in_specs=[whole, far, far],
        out_specs=[whole, far],
        out_shape=[
            jax.ShapeDtypeStruct((devices, 1, LANES), jnp.int32),
            jax.ShapeDtypeStruct((NB * SPAN, SUB, LANES), f32),
        ],
        scratch_shapes=[
            pltpu.VMEM((NB * SPAN, SUB, LANES), f32),
            pltpu.VMEM((wide, rows, LANES), f32),
            pltpu.VMEM(density.shape, bf16),
            pltpu.VMEM(swap.shape, bf16),
            pltpu.SemaphoreType.DMA((4,)),
            pltpu.SemaphoreType.DMA((4,)),
            pltpu.SemaphoreType.DMA((3,)),
            pltpu.SemaphoreType.DMA((4,)),
        ],
        compiler_params=pltpu.CompilerParams(
            collective_id=0, has_side_effects=True, vmem_limit_bytes=SPREAD_VMEM
        ),
        name="spread_and_cut",
    )(own_list, density, swap)


def pick_kernel(index_ref, tiles_ref, out_ref):
    per_step = out_ref.shape[0]
    first = pl.program_id(0) * per_step

    def one(n, carry):
        for pair in range(SLOTS // 2):
            halves = [tiles_ref[index_ref[2 * pair + h, first + n]] for h in range(2)]
            out_ref[n, 16 * pair : 16 * (pair + 1), :] = jnp.concatenate(halves, axis=0).astype(
                bf16
            )
        return carry

    lax.fori_loop(0, per_step, one, 0, unroll=8)


def pick_tiles(index, tiles):
    devices = index.shape[1]
    per_step = 64
    return pl.pallas_call(
        pick_kernel,
        grid_spec=pltpu.PrefetchScalarGridSpec(
            num_scalar_prefetch=1,
            grid=(devices // per_step,),
            in_specs=[pl.BlockSpec(memory_space=pltpu.VMEM)],
            out_specs=pl.BlockSpec((per_step, CHUNK, LANES), lambda i, index: (i, 0, 0)),
        ),
        out_shape=jax.ShapeDtypeStruct((devices, CHUNK, LANES), bf16),
        compiler_params=pltpu.CompilerParams(vmem_limit_bytes=PICK_VMEM),
        name="pick_tiles",
    )(index, tiles)


def pairings_kernel(g_ref, swap_ref, ps_ref, rs_ref, rows_ref, ps_rows, rs_rows):
    step = pl.program_id(1)
    rows_ref[...] = g_ref[0].astype(f32)
    swap = swap_ref[...]

    def spread(parts, target):
        out = times(jnp.concatenate(parts, axis=1), swap)
        for big in range(8):
            for s in range(4):
                target[big, pl.ds(4 * step + s, S, stride=S), :] = out[
                    S * big : S * (big + 1), LANES * s : LANES * (s + 1)
                ]

    spread(
        [
            jnp.concatenate(
                [rows_ref[pl.ds(4 * big + r, S, stride=S), :] for big in range(8)], axis=0
            ).astype(bf16)
            for r in range(4)
        ],
        ps_rows,
    )
    spread(
        [
            jnp.concatenate(
                [g_ref[0, S * (4 * big + p) : S * (4 * big + p + 1), :] for big in range(8)],
                axis=0,
            )
            for p in range(4)
        ],
        rs_rows,
    )

    @pl.when(step == pl.num_programs(1) - 1)
    def _():
        for big in range(8):
            lanes = slice(LANES * big, LANES * (big + 1))
            ps_ref[0, :, lanes] = ps_rows[big].astype(bf16)
            rs_ref[0, :, lanes] = rs_rows[big].astype(bf16)


def pairings(integrals, swap):
    count = integrals.shape[0]
    shape = jax.ShapeDtypeStruct(integrals.shape, bf16)
    block = pl.BlockSpec((1, AREA, AREA), lambda m, c: (m, 0, 0))
    return pl.pallas_call(
        pairings_kernel,
        grid=(count, AREA // LANES),
        in_specs=[
            pl.BlockSpec((1, AREA, LANES), lambda m, c: (m, 0, c)),
            pl.BlockSpec(swap.shape, lambda m, c: (0, 0)),
        ],
        out_specs=[block, block],
        out_shape=[shape, shape],
        scratch_shapes=[pltpu.VMEM((AREA, LANES), f32)]
        + [pltpu.VMEM((AREA // LANES, AREA, LANES), f32)] * 2,
        compiler_params=pltpu.CompilerParams(vmem_limit_bytes=PAIRINGS_VMEM),
        cost_estimate=pl.CostEstimate(
            flops=40_000_000_000, bytes_accessed=3 * 2 * count * AREA * AREA, transcendentals=0
        ),
        name="pairings",
    )(integrals, swap)


def digest_kernel(
    quarter_ref, recv_ref, g_ref, ps_ref, rs_ref, out_ref, rows_ref, made_ref, square_ref, sem
):
    count = g_ref.shape[0]
    slots = square_ref.shape[0]
    message = QUARTERS * CHUNK
    stride = message + 1
    squares = [ref.at[m] for m in range(count) for ref in (g_ref, ps_ref, rs_ref)]
    loads = [
        pltpu.make_async_copy(square, square_ref.at[n % slots], sem.at[n % slots])
        for n, square in enumerate(squares)
    ]
    for load in loads[: slots - 1]:
        load.start()

    def widen(x, carry):
        at = pl.multiple_of(x * message, message)
        rows_ref[pl.ds(x * stride, message), :] = recv_ref[pl.ds(at, message), :].astype(f32)
        return carry

    lax.fori_loop(0, P_SIZE, widen, 0)

    def fetch(quarter, slot):
        first = quarter * CHUNK + slot * SUB
        return jnp.concatenate(
            [
                rows_ref[pl.ds(first + c, P_SIZE, stride=stride), :].astype(bf16)
                for c in range(SUB)
            ],
            axis=1,
        )

    def put(quarter, slot, value):
        first = quarter * CHUNK + slot * SUB
        for c in range(SUB):
            made_ref[pl.ds(first + c, P_SIZE, stride=stride), :] = value[
                :, LANES * c : LANES * (c + 1)
            ]

    half = -0.5 * SCALE
    for n, load in enumerate(loads):
        q_i, q_j, q_k = (quarter_ref[3 * (n // 3) + role] for role in range(3))
        load.wait()
        if n + slots - 1 < len(loads):
            loads[n + slots - 1].start()
        square = square_ref[n % slots]
        if n % 3 == 0:
            put(q_i, 0, SCALE * times_turned(fetch(q_k, 4), square))
            put(q_k, 4, SCALE * times(fetch(q_i, 0), square))
        elif n % 3 == 1:
            put(q_i, 1, half * times_turned(fetch(q_j, 2), square))
            put(q_j, 2, half * times(fetch(q_i, 1), square))
        else:
            put(q_i, 5, half * times(fetch(q_j, 3), square))
            put(q_j, 3, half * times_turned(fetch(q_i, 5), square))

    def close_up(x, carry):
        at = pl.multiple_of(x * message, message)
        out_ref[pl.ds(at, message), :] = made_ref[pl.ds(x * stride, message), :]
        return carry

    lax.fori_loop(0, P_SIZE, close_up, 0)


def digest(quarters, received, integrals, ps, rs):
    rows = received.shape[0]
    slots = 4
    whole = pl.BlockSpec(memory_space=pltpu.VMEM)
    far = pl.BlockSpec(memory_space=pl.ANY)
    spaced = pltpu.VMEM((rows + P_SIZE, LANES), f32)
    return pl.pallas_call(
        digest_kernel,
        in_specs=[pl.BlockSpec(memory_space=pltpu.SMEM), whole, far, far, far],
        out_specs=whole,
        scratch_shapes=[
            spaced,
            spaced,
            pltpu.VMEM((slots, AREA, AREA), bf16),
            pltpu.SemaphoreType.DMA((slots,)),
        ],
        out_shape=jax.ShapeDtypeStruct((rows, LANES), f32),
        compiler_params=pltpu.CompilerParams(vmem_limit_bytes=DIGEST_VMEM),
        name="digest",
    )(quarters, received, integrals, ps, rs)


def finish_kernel(index_ref, recv_ref, orb_ref, swap_ref, out_ref, sums_ref, rows_ref, fock_ref):
    chains = sums_ref.shape[0]

    def clear(n, carry):
        sums_ref[:, pl.ds(SPAN * n, SPAN)] = jnp.zeros((chains, SPAN, SUB, LANES), f32)
        return carry

    lax.fori_loop(0, NB, clear, 0)

    def one(e, carry):
        for turn in range(SLOTS // chains):
            slots = range(turn * chains, (turn + 1) * chains)
            at = [index_ref[slot, e] for slot in slots]
            new = [
                sums_ref[chain, at[chain]] + recv_ref[e, SUB * slot : SUB * (slot + 1), :]
                for chain, slot in enumerate(slots)
            ]
            for chain in range(chains):
                sums_ref[chain, at[chain]] = new[chain]
        return carry

    lax.fori_loop(0, recv_ref.shape[0], one, 0, unroll=4)

    wide = rows_ref.shape[0]

    def columns(c, carry):
        lefts = []
        for w in range(wide):
            parts = []
            for b in range(4):
                tiles = pl.ds((4 * (wide * c + w) + b) * SPAN, SPAN)
                total = sums_ref[0, tiles]
                for chain in range(1, chains):
                    total = total + sums_ref[chain, tiles]
                parts.append((total * (1.0 / SCALE)).astype(bf16).reshape(SPAN * SUB, LANES))
            lefts.append(jnp.concatenate(parts, axis=1))
        out = times(jnp.concatenate(lefts, axis=0), swap_ref[...])
        for w in range(wide):
            for s in range(4):
                rows_ref[w, pl.ds(s, LANES, stride=4), :] = out[
                    LANES * w : LANES * (w + 1), LANES * s : LANES * (s + 1)
                ]
            at = pl.multiple_of((wide * c + w) * LANES, LANES)
            fock_ref[:, pl.ds(at, LANES)] = rows_ref[w].astype(bf16)
        return carry

    lax.fori_loop(0, NB // 4 // wide, columns, 0)
    out_ref[...] = times(fock_ref[...], orb_ref[...])


def finish(index, arrived, orbitals, swap, rows):
    basis, occupied = orbitals.shape
    chains = 3
    whole = pl.BlockSpec(memory_space=pltpu.VMEM)
    return pl.pallas_call(
        finish_kernel,
        in_specs=[pl.BlockSpec(memory_space=pltpu.SMEM), whole, whole, whole],
        out_specs=whole,
        scratch_shapes=[
            pltpu.VMEM((chains, NB * SPAN, SUB, LANES), f32),
            pltpu.VMEM((4, rows, LANES), f32),
            pltpu.VMEM((rows, basis), bf16),
        ],
        out_shape=jax.ShapeDtypeStruct((rows, occupied), f32),
        compiler_params=pltpu.CompilerParams(vmem_limit_bytes=32 << 20),
        name="finish",
    )(index, arrived, orbitals, swap)


def tile_index(lists, quarter):
    i, j, k, l = (lists[:, :, role] for role in range(4))
    low = quarter * SPAN
    of_i = i // SPAN == quarter
    of_j = j // SPAN == quarter
    of_k = k // SPAN == quarter

    def pick(mask, value):
        return jnp.sum(jnp.where(mask, value, 0), axis=0)

    return jnp.stack(
        [
            pick(of_i, j * SPAN + i - low),
            pick(of_i, k * SPAN + i - low),
            pick(of_j, l * SPAN + j - low),
            pick(of_j, k * SPAN + j - low),
            pick(of_k, l * SPAN + k - low),
            pick(of_i, l * SPAN + i - low),
        ]
    )


def per_device(integrals, quartets, density, orbitals):
    axes = ("quartet", "pert")
    devices = lax.axis_size("quartet") * lax.axis_size("pert")
    myself = lax.axis_index("quartet") * lax.axis_size("pert") + lax.axis_index("pert")
    quarter = myself % QUARTERS

    swap = group_swap()
    flat = jnp.pad(quartets.reshape(1, 1, GROUP * 4), ((0, 0), (0, 0), (0, LANES - GROUP * 4)))
    lists, tiles = spread_and_cut(flat, density, swap, devices)
    lists = lists.reshape(devices, LANES).T[: GROUP * 4].reshape(GROUP, 4, devices)
    index = tile_index(lists.transpose(0, 2, 1), quarter)

    outgoing = pick_tiles(index, tiles)
    received = lax.all_to_all(outgoing, axes, 0, 0, tiled=True)
    ps, rs = pairings(integrals, swap)
    quarters = (quartets[:, :3] // SPAN).reshape(-1)
    terms = digest(quarters, received.reshape(-1, LANES), integrals, ps, rs)
    leaving = terms.astype(f16).reshape(devices, CHUNK, LANES)
    landed = lax.all_to_all(leaving, axes, 0, 0, tiled=True)
    return finish(index, landed.astype(f32), orbitals, swap, density.shape[0])


def solution(mesh):
    placed = (
        P(("quartet", "pert"), None, None),
        P(("quartet", "pert"), None),
        P(("quartet", "pert"), None),
        P(),
    )
    return jax.shard_map(
        per_device,
        mesh=mesh,
        in_specs=placed,
        out_specs=P(("quartet", "pert"), None),
        check_vma=False,
    )
```

```python
import jax
import jax.numpy as jnp
import numpy as np
from jax import lax
from jax.experimental import pallas as pl
from jax.experimental.pallas import tpu as pltpu
from jax.sharding import PartitionSpec as P

P_SIZE = 64
S = 32
NB = 64
QUARTERS = 4
SPAN = NB // QUARTERS
GROUP = 4
SLOTS = 6
TILES = ((0, 1), (0, 2), (1, 3), (1, 2), (2, 3), (0, 3))
LANES = 128
SUB = 8
AREA = S * S
CHUNK = SLOTS * SUB
SCALE = 32.0

MESH = pl.DeviceIdType.MESH
EXCHANGE_VMEM = 46 << 20
DIGEST_VMEM = 44 << 20

f32 = jnp.float32
bf16 = jnp.bfloat16
f16 = jnp.float16


def group_swap():
    eye = np.eye(4 * LANES, dtype=np.float32)
    return jnp.asarray(eye.reshape(4, 4, S, 4 * LANES).transpose(1, 0, 2, 3).reshape(eye.shape), bf16)


def times(left, right):
    return jnp.dot(left, right, preferred_element_type=f32)


def times_turned(left, right):
    return lax.dot_general(left, right, (((1,), (1,)), ((), ())), preferred_element_type=f32)


def own_indices(quartet_ref, row_ref):
    members = [[quartet_ref[m, role] for role in range(4)] for m in range(GROUP)]
    for quarter in range(QUARTERS):
        low = quarter * SPAN

        def pick(row, column):
            total = jnp.int32(0)
            for member in members:
                within = jnp.logical_and(member[row] >= low, member[row] < low + SPAN)
                value = member[column] * SPAN + member[row] - low
                total = total + jnp.where(within, value, 0)
            return total

        for slot, (row, column) in enumerate(TILES):
            row_ref[0, 0, quarter * SLOTS + slot] = pick(row, column)
    for lane in range(QUARTERS * SLOTS, LANES):
        row_ref[0, 0, lane] = jnp.int32(0)


def exchange_kernel(
    quartet_ref,
    dens_from,
    swap_from,
    g_from,
    slots_ref,
    received_ref,
    ps_to,
    rs_to,
    row_ref,
    index_ref,
    lists_ref,
    tiles_ref,
    rows_ref,
    dens_ref,
    swap_ref,
    message_ref,
    g_ref,
    strip_ref,
    ps_rows,
    rs_rows,
    ps_ref,
    rs_ref,
    step_send,
    step_recv,
    own_sem,
    send_sem,
    recv_sem,
    g_sem,
    pair_sem,
):
    chip, core = lax.axis_index("quartet"), lax.axis_index("pert")
    x, y, z = chip % 4, (chip // 4) % 4, chip // 16
    me = 2 * chip + core
    devices = lists_ref.shape[0]

    steps = (
        (me, 1, [(chip, (core + 1) % 2)]),
        (2 * chip, 2, [(chip - x + (x + n) % 4, core) for n in range(1, 4)]),
        (8 * (chip // 4), 8, [(chip - 4 * y + 4 * ((y + n) % 4), core) for n in range(1, 4)]),
        (32 * z, 32, [(chip - 16 * z + 16 * ((z + n) % 8), core) for n in range(1, 8)]),
    )
    barrier = pltpu.get_barrier_semaphore()
    for _, _, partners in steps:
        for partner in partners:
            pl.semaphore_signal(barrier, inc=1, device_id=partner, device_id_type=MESH)
    fetches = (
        pltpu.make_async_copy(dens_from, dens_ref, own_sem.at[1]),
        pltpu.make_async_copy(swap_from, swap_ref, own_sem.at[2]),
    )
    for fetch in fetches:
        fetch.start()
    own_indices(quartet_ref, row_ref)
    own = pltpu.make_async_copy(row_ref, lists_ref.at[pl.ds(me, 1)], own_sem.at[0])
    own.start()

    wide = rows_ref.shape[0]

    def cut(n):
        parts = []
        for w in range(wide):
            columns = slice(LANES * (wide * n + w), LANES * (wide * n + w + 1))
            rows_ref[w] = dens_ref[:, columns].astype(f32)
            parts.append(
                jnp.concatenate(
                    [rows_ref[w, pl.ds(s, LANES, stride=4), :].astype(bf16) for s in range(4)],
                    axis=1,
                )
            )
        out = times(jnp.concatenate(parts, axis=0), swap_ref[...])
        for w in range(wide):
            for b in range(4):
                first = (4 * (wide * n + w) + b) * SPAN
                tiles_ref[first : first + SPAN] = out[
                    LANES * w : LANES * (w + 1), LANES * b : LANES * (b + 1)
                ].reshape(SPAN, SUB, LANES)

    own.wait()
    pl.semaphore_wait(barrier, sum(len(partners) for _, _, partners in steps))
    for n, (first, count, partners) in enumerate(steps):
        block = lists_ref.at[pl.ds(first, count)]
        for partner in partners:
            pltpu.make_async_remote_copy(
                src_ref=block,
                dst_ref=block,
                send_sem=step_send.at[n],
                recv_sem=step_recv.at[n],
                device_id=partner,
                device_id_type=MESH,
            ).start()
        if n == 0:
            for fetch in fetches:
                fetch.wait()
        cut(n)
        bytes_in = lists_ref.at[pl.ds(0, count * len(partners))]
        pltpu.make_async_copy(bytes_in, bytes_in, step_recv.at[n]).wait()

    to_scalars = pltpu.make_async_copy(lists_ref, index_ref, own_sem.at[0])
    to_scalars.start()

    count, area = g_from.shape[0], g_from.shape[1]
    strips = area // LANES

    def g_load(n):
        return pltpu.make_async_copy(
            g_from.at[n // strips, :, pl.ds(pl.multiple_of((n % strips) * LANES, LANES), LANES)],
            g_ref.at[n % 2],
            g_sem.at[n % 2],
        )

    g_load(0).start()
    to_scalars.wait()

    base = (me % QUARTERS) * SLOTS

    def pick(device):
        tiles = [tiles_ref[index_ref[device, 0, base + slot]] for slot in range(SLOTS)]
        for pair in range(SLOTS // 2):
            message_ref[device, 16 * pair : 16 * (pair + 1), :] = jnp.concatenate(
                tiles[2 * pair : 2 * pair + 2], axis=0
            ).astype(bf16)

    def send(n, carry):
        device = (me + n) % devices
        pick(device)
        pltpu.make_async_remote_copy(
            src_ref=message_ref.at[device],
            dst_ref=received_ref.at[me],
            send_sem=send_sem,
            recv_sem=recv_sem,
            device_id=(device // 2, device % 2),
            device_id_type=MESH,
        ).start()
        return carry

    lax.fori_loop(1, devices, send, 0)
    pick(me)
    keep = pltpu.make_async_copy(message_ref.at[me], received_ref.at[me], own_sem.at[1])
    keep.start()

    by_lane = lists_ref[...].reshape(devices, LANES).T
    slots = by_lane[:SLOTS]
    for quarter in range(1, QUARTERS):
        mine = by_lane[quarter * SLOTS : (quarter + 1) * SLOTS]
        slots = jnp.where(me % QUARTERS == quarter, mine, slots)
    slots_ref[...] = slots

    def stores(m):
        return (
            pltpu.make_async_copy(ps_ref, ps_to.at[m], pair_sem.at[0]),
            pltpu.make_async_copy(rs_ref, rs_to.at[m], pair_sem.at[1]),
        )

    def strip(n, carry):
        step = n % strips

        @pl.when(n + 1 < count * strips)
        def _():
            g_load(n + 1).start()

        g_load(n).wait()
        g = g_ref.at[n % 2]
        strip_ref[...] = g[...].astype(f32)
        swap = swap_ref[...]

        def spread(parts, target):
            out = times(jnp.concatenate(parts, axis=1), swap)
            for big in range(8):
                for s in range(4):
                    target[big, pl.ds(4 * step + s, S, stride=S), :] = out[
                        S * big : S * (big + 1), LANES * s : LANES * (s + 1)
                    ]

        spread(
            [
                jnp.concatenate(
                    [strip_ref[pl.ds(4 * big + r, S, stride=S), :] for big in range(8)], axis=0
                ).astype(bf16)
                for r in range(4)
            ],
            ps_rows,
        )
        spread(
            [
                jnp.concatenate(
                    [g[S * (4 * big + p) : S * (4 * big + p + 1), :] for big in range(8)], axis=0
                )
                for p in range(4)
            ],
            rs_rows,
        )

        @pl.when(step == strips - 1)
        def _():
            m = n // strips

            @pl.when(m > 0)
            def _():
                for store in stores(m - 1):
                    store.wait()

            for big in range(8):
                lanes = slice(LANES * big, LANES * (big + 1))
                ps_ref[:, lanes] = ps_rows[big].astype(bf16)
                rs_ref[:, lanes] = rs_rows[big].astype(bf16)
            for store in stores(m):
                store.start()

        return carry

    lax.fori_loop(0, count * strips, strip, 0)
    for store in stores(count - 1):
        store.wait()

    keep.wait()
    others = received_ref.at[pl.ds(0, devices - 1)]
    pltpu.make_async_copy(others, others, recv_sem).wait()
    pltpu.make_async_copy(others, others, send_sem).wait()
    for n, (_, count, partners) in enumerate(steps):
        bytes_out = lists_ref.at[pl.ds(0, count * len(partners))]
        pltpu.make_async_copy(bytes_out, bytes_out, step_send.at[n]).wait()


def exchange(quartets, density, swap, integrals, devices):
    rows, columns = density.shape
    count = integrals.shape[0]
    wide = columns // LANES // 4
    whole = pl.BlockSpec(memory_space=pltpu.VMEM)
    far = pl.BlockSpec(memory_space=pltpu.HBM)
    dma = pltpu.SemaphoreType.DMA
    return pl.pallas_call(
        exchange_kernel,
        in_specs=[pl.BlockSpec(memory_space=pltpu.SMEM), far, far, far],
        out_specs=[whole, whole, far, far],
        out_shape=[
            jax.ShapeDtypeStruct((SLOTS, devices), jnp.int32),
            jax.ShapeDtypeStruct((devices, CHUNK, LANES), bf16),
            jax.ShapeDtypeStruct((count, AREA, AREA), bf16),
            jax.ShapeDtypeStruct((count, AREA, AREA), bf16),
        ],
        scratch_shapes=[
            pltpu.SMEM((1, 1, LANES), jnp.int32),
            pltpu.SMEM((devices, 1, LANES), jnp.int32),
            pltpu.VMEM((devices, 1, LANES), jnp.int32),
            pltpu.VMEM((NB * SPAN, SUB, LANES), f32),
            pltpu.VMEM((wide, rows, LANES), f32),
            pltpu.VMEM(density.shape, bf16),
            pltpu.VMEM(swap.shape, bf16),
            pltpu.VMEM((devices, CHUNK, LANES), bf16),
            pltpu.VMEM((2, AREA, LANES), bf16),
            pltpu.VMEM((AREA, LANES), f32),
            pltpu.VMEM((AREA // LANES, AREA, LANES), f32),
            pltpu.VMEM((AREA // LANES, AREA, LANES), f32),
            pltpu.VMEM((AREA, AREA), bf16),
            pltpu.VMEM((AREA, AREA), bf16),
            dma((4,)),
            dma((4,)),
            dma((3,)),
            dma,
            dma,
            dma((2,)),
            dma((2,)),
        ],
        compiler_params=pltpu.CompilerParams(
            collective_id=0, has_side_effects=True, vmem_limit_bytes=EXCHANGE_VMEM
        ),
        name="exchange",
    )(quartets, density, swap, integrals)


def digest_kernel(
    quartet_ref, recv_ref, g_ref, ps_ref, rs_ref, out_ref, rows_ref, made_ref, square_ref, sem
):
    count = g_ref.shape[0]
    slots = square_ref.shape[0]
    message = QUARTERS * CHUNK
    stride = message + 1
    squares = [ref.at[m] for m in range(count) for ref in (g_ref, ps_ref, rs_ref)]
    loads = [
        pltpu.make_async_copy(square, square_ref.at[n % slots], sem.at[n % slots])
        for n, square in enumerate(squares)
    ]
    for load in loads[: slots - 1]:
        load.start()

    def widen(x, carry):
        at = pl.multiple_of(x * message, message)
        rows_ref[pl.ds(x * stride, message), :] = recv_ref[pl.ds(at, message), :].astype(f32)
        return carry

    lax.fori_loop(0, P_SIZE, widen, 0)

    def fetch(quarter, slot):
        first = quarter * CHUNK + slot * SUB
        return jnp.concatenate(
            [
                rows_ref[pl.ds(first + c, P_SIZE, stride=stride), :].astype(bf16)
                for c in range(SUB)
            ],
            axis=1,
        )

    def put(quarter, slot, value):
        first = quarter * CHUNK + slot * SUB
        for c in range(SUB):
            made_ref[pl.ds(first + c, P_SIZE, stride=stride), :] = value[
                :, LANES * c : LANES * (c + 1)
            ]

    half = -0.5 * SCALE
    for n, load in enumerate(loads):
        q_i, q_j, q_k = (quartet_ref[n // 3, role] // SPAN for role in range(3))
        load.wait()
        if n + slots - 1 < len(loads):
            loads[n + slots - 1].start()
        square = square_ref[n % slots]
        if n % 3 == 0:
            put(q_i, 0, SCALE * times_turned(fetch(q_k, 4), square))
            put(q_k, 4, SCALE * times(fetch(q_i, 0), square))
        elif n % 3 == 1:
            put(q_i, 1, half * times_turned(fetch(q_j, 2), square))
            put(q_j, 2, half * times(fetch(q_i, 1), square))
        else:
            put(q_i, 5, half * times(fetch(q_j, 3), square))
            put(q_j, 3, half * times_turned(fetch(q_i, 5), square))

    def close_up(x, carry):
        at = pl.multiple_of(x * message, message)
        out_ref[pl.ds(at, message), :] = made_ref[pl.ds(x * stride, message), :]
        return carry

    lax.fori_loop(0, P_SIZE, close_up, 0)


def digest(quartets, received, integrals, ps, rs):
    rows = received.shape[0]
    slots = 4
    whole = pl.BlockSpec(memory_space=pltpu.VMEM)
    far = pl.BlockSpec(memory_space=pltpu.HBM)
    spaced = pltpu.VMEM((rows + P_SIZE, LANES), f32)
    return pl.pallas_call(
        digest_kernel,
        in_specs=[pl.BlockSpec(memory_space=pltpu.SMEM), whole, far, far, far],
        out_specs=whole,
        scratch_shapes=[
            spaced,
            spaced,
            pltpu.VMEM((slots, AREA, AREA), bf16),
            pltpu.SemaphoreType.DMA((slots,)),
        ],
        out_shape=jax.ShapeDtypeStruct((rows, LANES), f32),
        compiler_params=pltpu.CompilerParams(vmem_limit_bytes=DIGEST_VMEM),
        name="digest",
    )(quartets, received, integrals, ps, rs)


def finish_kernel(index_ref, recv_ref, orb_ref, swap_ref, out_ref, sums_ref, rows_ref, fock_ref):
    chains = sums_ref.shape[0]

    def clear(n, carry):
        sums_ref[:, pl.ds(SPAN * n, SPAN)] = jnp.zeros((chains, SPAN, SUB, LANES), f32)
        return carry

    lax.fori_loop(0, NB, clear, 0)

    def one(e, carry):
        for turn in range(SLOTS // chains):
            slots = range(turn * chains, (turn + 1) * chains)
            at = [index_ref[slot, e] for slot in slots]
            new = [
                sums_ref[chain, at[chain]] + recv_ref[e, SUB * slot : SUB * (slot + 1), :]
                for chain, slot in enumerate(slots)
            ]
            for chain in range(chains):
                sums_ref[chain, at[chain]] = new[chain]
        return carry

    lax.fori_loop(0, recv_ref.shape[0], one, 0, unroll=4)

    wide = rows_ref.shape[0]

    def columns(c, carry):
        lefts = []
        for w in range(wide):
            parts = []
            for b in range(4):
                tiles = pl.ds((4 * (wide * c + w) + b) * SPAN, SPAN)
                total = sums_ref[0, tiles]
                for chain in range(1, chains):
                    total = total + sums_ref[chain, tiles]
                parts.append((total * (1.0 / SCALE)).astype(bf16).reshape(SPAN * SUB, LANES))
            lefts.append(jnp.concatenate(parts, axis=1))
        out = times(jnp.concatenate(lefts, axis=0), swap_ref[...])
        for w in range(wide):
            for s in range(4):
                rows_ref[w, pl.ds(s, LANES, stride=4), :] = out[
                    LANES * w : LANES * (w + 1), LANES * s : LANES * (s + 1)
                ]
            at = pl.multiple_of((wide * c + w) * LANES, LANES)
            fock_ref[:, pl.ds(at, LANES)] = rows_ref[w].astype(bf16)
        return carry

    lax.fori_loop(0, NB // 4 // wide, columns, 0)
    out_ref[...] = times(fock_ref[...], orb_ref[...])


def finish(index, arrived, orbitals, swap, rows):
    basis, occupied = orbitals.shape
    chains = 3
    whole = pl.BlockSpec(memory_space=pltpu.VMEM)
    return pl.pallas_call(
        finish_kernel,
        in_specs=[pl.BlockSpec(memory_space=pltpu.SMEM), whole, whole, whole],
        out_specs=whole,
        scratch_shapes=[
            pltpu.VMEM((chains, NB * SPAN, SUB, LANES), f32),
            pltpu.VMEM((4, rows, LANES), f32),
            pltpu.VMEM((rows, basis), bf16),
        ],
        out_shape=jax.ShapeDtypeStruct((rows, occupied), f32),
        compiler_params=pltpu.CompilerParams(vmem_limit_bytes=32 << 20),
        name="finish",
    )(index, arrived, orbitals, swap)


def per_device(integrals, quartets, density, orbitals):
    axes = ("quartet", "pert")
    devices = lax.axis_size("quartet") * lax.axis_size("pert")
    swap = group_swap()
    index, received, ps, rs = exchange(quartets, density, swap, integrals, devices)
    terms = digest(quartets, received.reshape(-1, LANES), integrals, ps, rs)
    leaving = terms.astype(f16).reshape(devices, CHUNK, LANES)
    landed = lax.all_to_all(leaving, axes, 0, 0, tiled=True)
    return finish(index, landed.astype(f32), orbitals, swap, density.shape[0])


def solution(mesh):
    placed = (
        P(("quartet", "pert"), None, None),
        P(("quartet", "pert"), None),
        P(("quartet", "pert"), None),
        P(),
    )
    return jax.shard_map(
        per_device,
        mesh=mesh,
        in_specs=placed,
        out_specs=P(("quartet", "pert"), None),
        check_vma=False,
    )
```

```python
import jax
import jax.numpy as jnp
import numpy as np
from jax import lax
from jax.experimental import pallas as pl
from jax.experimental.pallas import tpu as pltpu
from jax.sharding import PartitionSpec as P

P_SIZE = 64
S = 32
NB = 64
QUARTERS = 4
PARTS = ((2, 3, 4, 5), (0, 1))
SPAN = NB // QUARTERS
GROUP = 4
SLOTS = 6
TILES = ((0, 1), (0, 2), (1, 3), (1, 2), (2, 3), (0, 3))
LANES = 128
SUB = 8
AREA = S * S
CHUNK = SLOTS * SUB
SCALE = 32.0

MESH = pl.DeviceIdType.MESH
EXCHANGE_VMEM = 54 << 20

f32 = jnp.float32
bf16 = jnp.bfloat16
f16 = jnp.float16


def group_swap():
    eye = np.eye(4 * LANES, dtype=np.float32)
    return jnp.asarray(eye.reshape(4, 4, S, 4 * LANES).transpose(1, 0, 2, 3).reshape(eye.shape), bf16)


def times(left, right):
    return jnp.dot(left, right, preferred_element_type=f32)


def times_turned(left, right):
    return lax.dot_general(left, right, (((1,), (1,)), ((), ())), preferred_element_type=f32)


def own_indices(quartet_ref, row_ref):
    members = [[quartet_ref[m, role] for role in range(4)] for m in range(GROUP)]
    for quarter in range(QUARTERS):
        low = quarter * SPAN

        def pick(row, column):
            total = jnp.int32(0)
            for member in members:
                within = jnp.logical_and(member[row] >= low, member[row] < low + SPAN)
                value = member[column] * SPAN + member[row] - low
                total = total + jnp.where(within, value, 0)
            return total

        for slot, (row, column) in enumerate(TILES):
            row_ref[0, 0, quarter * SLOTS + slot] = pick(row, column)
    for lane in range(QUARTERS * SLOTS, LANES):
        row_ref[0, 0, lane] = jnp.int32(0)


def exchange_kernel(
    quartet_ref,
    dens_from,
    swap_from,
    g_from,
    slots_ref,
    out_ref,
    row_ref,
    index_ref,
    lists_ref,
    dens_ref,
    swap_ref,
    message_ref,
    first_ref,
    last_ref,
    tiles_ref,
    g_ref,
    ps_ref,
    rs_ref,
    strip_ref,
    one_ref,
    two_ref,
    step_send,
    step_recv,
    own_sem,
    send_sem,
    recv_sem,
    store_sem,
):
    parts_ref = (first_ref, last_ref)
    chip, core = lax.axis_index("quartet"), lax.axis_index("pert")
    x, y, z = chip % 4, (chip // 4) % 4, chip // 16
    me = 2 * chip + core
    devices = lists_ref.shape[0]

    steps = (
        (me, 1, [(chip, (core + 1) % 2)]),
        (2 * chip, 2, [(chip - x + (x + n) % 4, core) for n in range(1, 4)]),
        (8 * (chip // 4), 8, [(chip - 4 * y + 4 * ((y + n) % 4), core) for n in range(1, 4)]),
        (32 * z, 32, [(chip - 16 * z + 16 * ((z + n) % 8), core) for n in range(1, 8)]),
    )
    barrier = pltpu.get_barrier_semaphore()
    for _, _, partners in steps:
        for partner in partners:
            pl.semaphore_signal(barrier, inc=1, device_id=partner, device_id_type=MESH)
    fetches = (
        pltpu.make_async_copy(dens_from, dens_ref, own_sem.at[1]),
        pltpu.make_async_copy(swap_from, swap_ref, own_sem.at[2]),
    )
    for fetch in fetches:
        fetch.start()
    g_load = pltpu.make_async_copy(g_from, g_ref, own_sem.at[3])
    own_indices(quartet_ref, row_ref)
    own = pltpu.make_async_copy(row_ref, lists_ref.at[pl.ds(me, 1)], own_sem.at[0])
    own.start()

    tall = dens_ref.shape[0]
    wide = dens_ref.shape[1] // LANES // len(steps)

    def cut(n):
        parts = []
        for w in range(wide):
            columns = slice(LANES * (wide * n + w), LANES * (wide * n + w + 1))
            one_ref[tall * w : tall * (w + 1), :] = dens_ref[:, columns].astype(f32)
            parts.append(
                jnp.concatenate(
                    [
                        one_ref[pl.ds(tall * w + s, LANES, stride=4), :].astype(bf16)
                        for s in range(4)
                    ],
                    axis=1,
                )
            )
        out = times(jnp.concatenate(parts, axis=0), swap_ref[...])
        for w in range(wide):
            for b in range(4):
                first = (4 * (wide * n + w) + b) * SPAN
                tiles_ref[first : first + SPAN] = out[
                    LANES * w : LANES * (w + 1), LANES * b : LANES * (b + 1)
                ].reshape(SPAN, SUB, LANES)

    own.wait()
    pl.semaphore_wait(barrier, sum(len(partners) for _, _, partners in steps))
    for n, (first, count, partners) in enumerate(steps):
        block = lists_ref.at[pl.ds(first, count)]
        for partner in partners:
            pltpu.make_async_remote_copy(
                src_ref=block,
                dst_ref=block,
                send_sem=step_send.at[n],
                recv_sem=step_recv.at[n],
                device_id=partner,
                device_id_type=MESH,
            ).start()
        if n == 0:
            for fetch in fetches:
                fetch.wait()
        cut(n)
        bytes_in = lists_ref.at[pl.ds(0, count * len(partners))]
        pltpu.make_async_copy(bytes_in, bytes_in, step_recv.at[n]).wait()

    to_scalars = pltpu.make_async_copy(lists_ref, index_ref, own_sem.at[0])
    to_scalars.start()
    g_load.start()
    to_scalars.wait()

    base = (me % QUARTERS) * SLOTS

    def pick(device, slots):
        for slot in slots[::2]:
            tiles = [tiles_ref[index_ref[device, 0, base + slot + half]] for half in range(2)]
            message_ref[device, SUB * slot : SUB * (slot + 2), :] = jnp.concatenate(
                tiles, axis=0
            ).astype(bf16)

    def send_part(part):
        slots = PARTS[part]
        rows = pl.ds(SUB * slots[0], SUB * len(slots))

        def send(n, carry):
            device = (me + n) % devices
            pick(device, slots)
            pltpu.make_async_remote_copy(
                src_ref=message_ref.at[device, rows],
                dst_ref=parts_ref[part].at[me],
                send_sem=send_sem.at[part],
                recv_sem=recv_sem.at[part],
                device_id=(device // 2, device % 2),
                device_id_type=MESH,
            ).start()
            return carry

        lax.fori_loop(1, devices, send, 0)
        pick(me, slots)
        pltpu.make_async_copy(
            message_ref.at[me, rows], parts_ref[part].at[me], own_sem.at[1 + part]
        ).start()

    for part in range(len(PARTS)):
        send_part(part)

    by_lane = lists_ref[...].reshape(devices, LANES).T
    slots = by_lane[:SLOTS]
    for quarter in range(1, QUARTERS):
        mine = by_lane[quarter * SLOTS : (quarter + 1) * SLOTS]
        slots = jnp.where(me % QUARTERS == quarter, mine, slots)
    slots_ref[...] = slots

    g_load.wait()
    count, area = g_ref.shape[0], g_ref.shape[1]
    strips = area // LANES
    gap = S + 1

    def strip(n, carry):
        m, step = n // strips, n % strips
        lanes = pl.ds(pl.multiple_of(step * LANES, LANES), LANES)
        swap = swap_ref[...]
        blocks = [g_ref[m, S * p : S * (p + 1), lanes] for p in range(S)]
        for p in range(S):
            strip_ref[gap * p : gap * p + S, :] = blocks[p].astype(f32)

        def spread(parts, target):
            out = times(jnp.concatenate(parts, axis=1), swap)
            for big in range(strips):
                for s in range(4):
                    first = gap * S * big + 4 * step + s
                    target[pl.ds(first, S, stride=gap), :] = out[
                        S * big : S * (big + 1), LANES * s : LANES * (s + 1)
                    ]

        spread(
            [
                jnp.concatenate(
                    [strip_ref[pl.ds(4 * big + r, S, stride=gap), :] for big in range(strips)],
                    axis=0,
                ).astype(bf16)
                for r in range(4)
            ],
            one_ref,
        )
        spread(
            [
                jnp.concatenate([blocks[4 * big + p] for big in range(strips)], axis=0)
                for p in range(4)
            ],
            two_ref,
        )

        @pl.when(step == strips - 1)
        def _():
            def close_up(big, carry):
                lanes = pl.ds(pl.multiple_of(big * LANES, LANES), LANES)
                for row in range(S):
                    first = gap * S * big + gap * row
                    rows = slice(S * row, S * (row + 1))
                    ps_ref[m, rows, lanes] = one_ref[pl.ds(first, S), :].astype(bf16)
                    rs_ref[m, rows, lanes] = two_ref[pl.ds(first, S), :].astype(bf16)
                return carry

            lax.fori_loop(0, strips, close_up, 0)

        return carry

    lax.fori_loop(0, count * strips, strip, 0)

    message = QUARTERS * CHUNK
    stride = message + 1
    quarters = [[quartet_ref[m, role] // SPAN for role in range(3)] for m in range(GROUP)]

    def arrive(part):
        rows = pl.ds(SUB * PARTS[part][0], SUB * len(PARTS[part]))
        pltpu.make_async_copy(
            message_ref.at[me, rows], parts_ref[part].at[me], own_sem.at[1 + part]
        ).wait()
        others = parts_ref[part].at[pl.ds(0, devices - 1)]
        pltpu.make_async_copy(others, others, recv_sem.at[part]).wait()

        def widen(pert, carry):
            for m in range(GROUP):
                for n, slot in enumerate(PARTS[part]):
                    device = QUARTERS * pert + quarters[m][TILES[slot][0]]
                    at = pert * stride + m * CHUNK + slot * SUB
                    one_ref[pl.ds(at, SUB), :] = parts_ref[part][
                        device, SUB * n : SUB * (n + 1), :
                    ].astype(f32)
            return carry

        lax.fori_loop(0, P_SIZE, widen, 0)

    def fetch_tiles(m, slot):
        first = m * CHUNK + slot * SUB
        return jnp.concatenate(
            [
                one_ref[pl.ds(first + c, P_SIZE, stride=stride), :].astype(bf16)
                for c in range(SUB)
            ],
            axis=1,
        )

    def put(m, slot, value):
        first = m * CHUNK + slot * SUB
        for c in range(SUB):
            two_ref[pl.ds(first + c, P_SIZE, stride=stride), :] = value[
                :, LANES * c : LANES * (c + 1)
            ]

    half = -0.5 * SCALE

    def first_products(m, carry):
        put(m, 1, half * times_turned(fetch_tiles(m, 2), ps_ref[m]))
        put(m, 5, half * times(fetch_tiles(m, 3), rs_ref[m]))
        put(m, 0, SCALE * times_turned(fetch_tiles(m, 4), g_ref[m]))
        put(m, 3, half * times_turned(fetch_tiles(m, 5), rs_ref[m]))
        return carry

    def last_products(m, carry):
        put(m, 4, SCALE * times(fetch_tiles(m, 0), g_ref[m]))
        put(m, 2, half * times(fetch_tiles(m, 1), ps_ref[m]))
        return carry

    arrive(0)
    lax.fori_loop(0, count, first_products, 0)
    arrive(1)
    lax.fori_loop(0, count, last_products, 0)

    def close_up(pert, carry):
        to = pl.multiple_of(pert * message, message)
        one_ref[pl.ds(to, message), :] = two_ref[pl.ds(pert * stride, message), :]
        return carry

    leaves = []
    share = P_SIZE // store_sem.shape[0]
    for n in range(store_sem.shape[0]):
        lax.fori_loop(n * share, (n + 1) * share, close_up, 0)
        rows = pl.ds(n * share * message, share * message)
        leaves.append(pltpu.make_async_copy(one_ref.at[rows], out_ref.at[rows], store_sem.at[n]))
        leaves[n].start()
    for leave in leaves:
        leave.wait()

    for part in range(len(PARTS)):
        others = parts_ref[part].at[pl.ds(0, devices - 1)]
        pltpu.make_async_copy(others, others, send_sem.at[part]).wait()
    for n, (_, count, partners) in enumerate(steps):
        bytes_out = lists_ref.at[pl.ds(0, count * len(partners))]
        pltpu.make_async_copy(bytes_out, bytes_out, step_send.at[n]).wait()


def exchange(quartets, density, swap, integrals, devices):
    whole = pl.BlockSpec(memory_space=pltpu.VMEM)
    far = pl.BlockSpec(memory_space=pltpu.HBM)
    dma = pltpu.SemaphoreType.DMA
    spaced = pltpu.VMEM((devices * CHUNK + P_SIZE, LANES), f32)
    return pl.pallas_call(
        exchange_kernel,
        in_specs=[pl.BlockSpec(memory_space=pltpu.SMEM), far, far, far],
        out_specs=[whole, far],
        out_shape=[
            jax.ShapeDtypeStruct((SLOTS, devices), jnp.int32),
            jax.ShapeDtypeStruct((devices * CHUNK, LANES), f32),
        ],
        scratch_shapes=[
            pltpu.SMEM((1, 1, LANES), jnp.int32),
            pltpu.SMEM((devices, 1, LANES), jnp.int32),
            pltpu.VMEM((devices, 1, LANES), jnp.int32),
            pltpu.VMEM(density.shape, bf16),
            pltpu.VMEM(swap.shape, bf16),
            pltpu.VMEM((devices, CHUNK, LANES), bf16),
            pltpu.VMEM((devices, SUB * len(PARTS[0]), LANES), bf16),
            pltpu.VMEM((devices, SUB * len(PARTS[1]), LANES), bf16),
            pltpu.VMEM((NB * SPAN, SUB, LANES), f32),
            pltpu.VMEM(integrals.shape, bf16),
            pltpu.VMEM(integrals.shape, bf16),
            pltpu.VMEM(integrals.shape, bf16),
            pltpu.VMEM((S * (S + 1), LANES), f32),
            spaced,
            spaced,
            dma((4,)),
            dma((4,)),
            dma((4,)),
            dma((2,)),
            dma((2,)),
            dma((8,)),
        ],
        compiler_params=pltpu.CompilerParams(
            collective_id=0, has_side_effects=True, vmem_limit_bytes=EXCHANGE_VMEM
        ),
        name="exchange",
    )(quartets, density, swap, integrals)


def order_kernel(quartet_ref, made_ref, out_ref):
    message = QUARTERS * CHUNK
    first = pl.program_id(0) * (made_ref.shape[0] // message)
    quarters = [[quartet_ref[m, role] // SPAN for role in range(3)] for m in range(GROUP)]

    def one(pert, carry):
        for m in range(GROUP):
            for slot in range(SLOTS):
                quarter = quarters[m][TILES[slot][0]]
                to = (first + pert) * message + quarter * CHUNK + slot * SUB
                to = pl.multiple_of(to, SUB)
                at = pl.multiple_of(pert * message + m * CHUNK + slot * SUB, SUB)
                out_ref[pl.ds(to, SUB), :] = made_ref[pl.ds(at, SUB), :]
        return carry

    lax.fori_loop(0, made_ref.shape[0] // message, one, 0)


def by_owner(quartets, made):
    block = pl.BlockSpec((8 * QUARTERS * CHUNK, LANES), lambda i, quartets: (i, 0))
    return pl.pallas_call(
        order_kernel,
        grid_spec=pltpu.PrefetchScalarGridSpec(
            num_scalar_prefetch=1,
            grid=(P_SIZE // 8,),
            in_specs=[block],
            out_specs=pl.BlockSpec(memory_space=pltpu.VMEM),
        ),
        out_shape=jax.ShapeDtypeStruct(made.shape, f32),
        compiler_params=pltpu.CompilerParams(vmem_limit_bytes=46 << 20),
        name="by_owner",
    )(quartets, made)


def finish_kernel(index_ref, recv_ref, orb_ref, swap_ref, out_ref, sums_ref, rows_ref, fock_ref):
    chains = sums_ref.shape[0]

    def clear(n, carry):
        sums_ref[:, pl.ds(SPAN * n, SPAN)] = jnp.zeros((chains, SPAN, SUB, LANES), f32)
        return carry

    lax.fori_loop(0, NB, clear, 0)

    def one(e, carry):
        for turn in range(SLOTS // chains):
            slots = range(turn * chains, (turn + 1) * chains)
            at = [index_ref[slot, e] for slot in slots]
            new = [
                sums_ref[chain, at[chain]] + recv_ref[e, SUB * slot : SUB * (slot + 1), :]
                for chain, slot in enumerate(slots)
            ]
            for chain in range(chains):
                sums_ref[chain, at[chain]] = new[chain]
        return carry

    lax.fori_loop(0, recv_ref.shape[0], one, 0, unroll=4)

    wide = rows_ref.shape[0]

    def columns(c, carry):
        lefts = []
        for w in range(wide):
            parts = []
            for b in range(4):
                tiles = pl.ds((4 * (wide * c + w) + b) * SPAN, SPAN)
                total = sums_ref[0, tiles]
                for chain in range(1, chains):
                    total = total + sums_ref[chain, tiles]
                parts.append((total * (1.0 / SCALE)).astype(bf16).reshape(SPAN * SUB, LANES))
            lefts.append(jnp.concatenate(parts, axis=1))
        out = times(jnp.concatenate(lefts, axis=0), swap_ref[...])
        for w in range(wide):
            for s in range(4):
                rows_ref[w, pl.ds(s, LANES, stride=4), :] = out[
                    LANES * w : LANES * (w + 1), LANES * s : LANES * (s + 1)
                ]
            at = pl.multiple_of((wide * c + w) * LANES, LANES)
            fock_ref[:, pl.ds(at, LANES)] = rows_ref[w].astype(bf16)
        return carry

    lax.fori_loop(0, NB // 4 // wide, columns, 0)
    out_ref[...] = times(fock_ref[...], orb_ref[...])


def finish(index, arrived, orbitals, swap, rows):
    basis, occupied = orbitals.shape
    chains = 3
    whole = pl.BlockSpec(memory_space=pltpu.VMEM)
    return pl.pallas_call(
        finish_kernel,
        in_specs=[pl.BlockSpec(memory_space=pltpu.SMEM), whole, whole, whole],
        out_specs=whole,
        scratch_shapes=[
            pltpu.VMEM((chains, NB * SPAN, SUB, LANES), f32),
            pltpu.VMEM((4, rows, LANES), f32),
            pltpu.VMEM((rows, basis), bf16),
        ],
        out_shape=jax.ShapeDtypeStruct((rows, occupied), f32),
        compiler_params=pltpu.CompilerParams(vmem_limit_bytes=32 << 20),
        name="finish",
    )(index, arrived, orbitals, swap)


def per_device(integrals, quartets, density, orbitals):
    axes = ("quartet", "pert")
    devices = lax.axis_size("quartet") * lax.axis_size("pert")
    swap = group_swap()
    index, made = exchange(quartets, density, swap, integrals, devices)
    terms = by_owner(quartets, made)
    leaving = terms.astype(f16).reshape(devices, CHUNK, LANES)
    landed = lax.all_to_all(leaving, axes, 0, 0, tiled=True)
    return finish(index, landed.astype(f32), orbitals, swap, density.shape[0])


def solution(mesh):
    placed = (
        P(("quartet", "pert"), None, None),
        P(("quartet", "pert"), None),
        P(("quartet", "pert"), None),
        P(),
    )
    return jax.shard_map(
        per_device,
        mesh=mesh,
        in_specs=placed,
        out_specs=P(("quartet", "pert"), None),
        check_vma=False,
    )
```

```python
import jax
import jax.numpy as jnp
import numpy as np
from jax import lax
from jax.experimental import pallas as pl
from jax.experimental.pallas import tpu as pltpu
from jax.sharding import PartitionSpec as P

P_SIZE = 64
S = 32
NB = 64
QUARTERS = 4
PARTS = ((2, 3, 4, 5), (0, 1))
SPAN = NB // QUARTERS
GROUP = 4
SLOTS = 6
TILES = ((0, 1), (0, 2), (1, 3), (1, 2), (2, 3), (0, 3))
LANES = 128
SUB = 8
AREA = S * S
CHUNK = SLOTS * SUB
SCALE = 32.0

MESH = pl.DeviceIdType.MESH
EXCHANGE_VMEM = 54 << 20

f32 = jnp.float32
bf16 = jnp.bfloat16
f16 = jnp.float16


def group_swap():
    eye = np.eye(4 * LANES, dtype=np.float32)
    return jnp.asarray(eye.reshape(4, 4, S, 4 * LANES).transpose(1, 0, 2, 3).reshape(eye.shape), bf16)


def times(left, right):
    return jnp.dot(left, right, preferred_element_type=f32)


def times_turned(left, right):
    return lax.dot_general(left, right, (((1,), (1,)), ((), ())), preferred_element_type=f32)


def own_indices(quartet_ref, row_ref):
    members = [[quartet_ref[m, role] for role in range(4)] for m in range(GROUP)]
    for quarter in range(QUARTERS):
        low = quarter * SPAN

        def pick(row, column):
            total = jnp.int32(0)
            for member in members:
                within = jnp.logical_and(member[row] >= low, member[row] < low + SPAN)
                value = member[column] * SPAN + member[row] - low
                total = total + jnp.where(within, value, 0)
            return total

        for slot, (row, column) in enumerate(TILES):
            row_ref[0, 0, quarter * SLOTS + slot] = pick(row, column)
    for lane in range(QUARTERS * SLOTS, LANES):
        row_ref[0, 0, lane] = jnp.int32(0)


def exchange_kernel(
    quartet_ref,
    dens_from,
    swap_from,
    g_from,
    slots_ref,
    out_ref,
    row_ref,
    index_ref,
    lists_ref,
    dens_ref,
    swap_ref,
    message_ref,
    first_ref,
    last_ref,
    tiles_ref,
    g_ref,
    ps_ref,
    rs_ref,
    strip_ref,
    one_ref,
    two_ref,
    step_send,
    step_recv,
    own_sem,
    send_sem,
    recv_sem,
    store_sem,
):
    parts_ref = (first_ref, last_ref)
    chip, core = lax.axis_index("quartet"), lax.axis_index("pert")
    x, y, z = chip % 4, (chip // 4) % 4, chip // 16
    me = 2 * chip + core
    devices = lists_ref.shape[0]

    steps = (
        (me, 1, [(chip, (core + 1) % 2)]),
        (2 * chip, 2, [(chip - x + (x + n) % 4, core) for n in range(1, 4)]),
        (8 * (chip // 4), 8, [(chip - 4 * y + 4 * ((y + n) % 4), core) for n in range(1, 4)]),
        (32 * z, 32, [(chip - 16 * z + 16 * ((z + n) % 8), core) for n in range(1, 8)]),
    )
    barrier = pltpu.get_barrier_semaphore()
    for _, _, partners in steps:
        for partner in partners:
            pl.semaphore_signal(barrier, inc=1, device_id=partner, device_id_type=MESH)
    fetches = (
        pltpu.make_async_copy(dens_from, dens_ref, own_sem.at[1]),
        pltpu.make_async_copy(swap_from, swap_ref, own_sem.at[2]),
    )
    for fetch in fetches:
        fetch.start()
    g_load = pltpu.make_async_copy(g_from, g_ref, own_sem.at[3])
    own_indices(quartet_ref, row_ref)
    own = pltpu.make_async_copy(row_ref, lists_ref.at[pl.ds(me, 1)], own_sem.at[0])
    own.start()

    tall = dens_ref.shape[0]
    wide = dens_ref.shape[1] // LANES // len(steps)

    def cut(n):
        parts = []
        for w in range(wide):
            columns = slice(LANES * (wide * n + w), LANES * (wide * n + w + 1))
            one_ref[tall * w : tall * (w + 1), :] = dens_ref[:, columns].astype(f32)
            parts.append(
                jnp.concatenate(
                    [
                        one_ref[pl.ds(tall * w + s, LANES, stride=4), :].astype(bf16)
                        for s in range(4)
                    ],
                    axis=1,
                )
            )
        out = times(jnp.concatenate(parts, axis=0), swap_ref[...])
        for w in range(wide):
            for b in range(4):
                first = (4 * (wide * n + w) + b) * SPAN
                tiles_ref[first : first + SPAN] = out[
                    LANES * w : LANES * (w + 1), LANES * b : LANES * (b + 1)
                ].reshape(SPAN, SUB, LANES)

    own.wait()
    pl.semaphore_wait(barrier, sum(len(partners) for _, _, partners in steps))
    for n, (first, count, partners) in enumerate(steps):
        block = lists_ref.at[pl.ds(first, count)]
        for partner in partners:
            pltpu.make_async_remote_copy(
                src_ref=block,
                dst_ref=block,
                send_sem=step_send.at[n],
                recv_sem=step_recv.at[n],
                device_id=partner,
                device_id_type=MESH,
            ).start()
        if n == 0:
            for fetch in fetches:
                fetch.wait()
        cut(n)
        bytes_in = lists_ref.at[pl.ds(0, count * len(partners))]
        pltpu.make_async_copy(bytes_in, bytes_in, step_recv.at[n]).wait()

    to_scalars = pltpu.make_async_copy(lists_ref, index_ref, own_sem.at[0])
    to_scalars.start()
    g_load.start()
    to_scalars.wait()

    base = (me % QUARTERS) * SLOTS

    def pick(device, slots):
        for slot in slots[::2]:
            tiles = [tiles_ref[index_ref[device, 0, base + slot + half]] for half in range(2)]
            message_ref[device, SUB * slot : SUB * (slot + 2), :] = jnp.concatenate(
                tiles, axis=0
            ).astype(bf16)

    def send_part(part):
        slots = PARTS[part]
        rows = pl.ds(SUB * slots[0], SUB * len(slots))

        def send(n, carry):
            device = (me + n) % devices
            pick(device, slots)
            pltpu.make_async_remote_copy(
                src_ref=message_ref.at[device, rows],
                dst_ref=parts_ref[part].at[me],
                send_sem=send_sem.at[part],
                recv_sem=recv_sem.at[part],
                device_id=(device // 2, device % 2),
                device_id_type=MESH,
            ).start()
            return carry

        lax.fori_loop(1, devices, send, 0)
        pick(me, slots)
        pltpu.make_async_copy(
            message_ref.at[me, rows], parts_ref[part].at[me], own_sem.at[1 + part]
        ).start()

    for part in range(len(PARTS)):
        send_part(part)

    by_lane = lists_ref[...].reshape(devices, LANES).T
    slots = by_lane[:SLOTS]
    for quarter in range(1, QUARTERS):
        mine = by_lane[quarter * SLOTS : (quarter + 1) * SLOTS]
        slots = jnp.where(me % QUARTERS == quarter, mine, slots)
    slots_ref[...] = slots

    g_load.wait()
    count, area = g_ref.shape[0], g_ref.shape[1]
    strips = area // LANES
    gap = S + 1

    def strip(n, carry):
        m, step = n // strips, n % strips
        lanes = pl.ds(pl.multiple_of(step * LANES, LANES), LANES)
        swap = swap_ref[...]
        blocks = [g_ref[m, S * p : S * (p + 1), lanes] for p in range(S)]
        for p in range(S):
            strip_ref[gap * p : gap * p + S, :] = blocks[p].astype(f32)

        def spread(parts, target):
            out = times(jnp.concatenate(parts, axis=1), swap)
            for big in range(strips):
                for s in range(4):
                    first = gap * S * big + 4 * step + s
                    target[pl.ds(first, S, stride=gap), :] = out[
                        S * big : S * (big + 1), LANES * s : LANES * (s + 1)
                    ]

        spread(
            [
                jnp.concatenate(
                    [strip_ref[pl.ds(4 * big + r, S, stride=gap), :] for big in range(strips)],
                    axis=0,
                ).astype(bf16)
                for r in range(4)
            ],
            one_ref,
        )
        spread(
            [
                jnp.concatenate([blocks[4 * big + p] for big in range(strips)], axis=0)
                for p in range(4)
            ],
            two_ref,
        )

        @pl.when(step == strips - 1)
        def _():
            def close_up(big, carry):
                lanes = pl.ds(pl.multiple_of(big * LANES, LANES), LANES)
                for row in range(S):
                    first = gap * S * big + gap * row
                    rows = slice(S * row, S * (row + 1))
                    ps_ref[m, rows, lanes] = one_ref[pl.ds(first, S), :].astype(bf16)
                    rs_ref[m, rows, lanes] = two_ref[pl.ds(first, S), :].astype(bf16)
                return carry

            lax.fori_loop(0, strips, close_up, 0)

        return carry

    lax.fori_loop(0, count * strips, strip, 0)

    message = QUARTERS * CHUNK
    stride = message + 1
    quarters = [[quartet_ref[m, role] // SPAN for role in range(3)] for m in range(GROUP)]

    def arrive(part):
        rows = pl.ds(SUB * PARTS[part][0], SUB * len(PARTS[part]))
        pltpu.make_async_copy(
            message_ref.at[me, rows], parts_ref[part].at[me], own_sem.at[1 + part]
        ).wait()
        others = parts_ref[part].at[pl.ds(0, devices - 1)]
        pltpu.make_async_copy(others, others, recv_sem.at[part]).wait()

        def widen(pert, carry):
            for m in range(GROUP):
                for n, slot in enumerate(PARTS[part]):
                    device = QUARTERS * pert + quarters[m][TILES[slot][0]]
                    at = pert * stride + m * CHUNK + slot * SUB
                    one_ref[pl.ds(at, SUB), :] = parts_ref[part][
                        device, SUB * n : SUB * (n + 1), :
                    ].astype(f32)
            return carry

        lax.fori_loop(0, P_SIZE, widen, 0)

    def fetch_tiles(m, slot):
        first = m * CHUNK + slot * SUB
        return jnp.concatenate(
            [
                one_ref[pl.ds(first + c, P_SIZE, stride=stride), :].astype(bf16)
                for c in range(SUB)
            ],
            axis=1,
        )

    def put(m, slot, value):
        first = m * CHUNK + slot * SUB
        for c in range(SUB):
            two_ref[pl.ds(first + c, P_SIZE, stride=stride), :] = value[
                :, LANES * c : LANES * (c + 1)
            ]

    half = -0.5 * SCALE

    def first_products(m, carry):
        put(m, 1, half * times_turned(fetch_tiles(m, 2), ps_ref[m]))
        put(m, 5, half * times(fetch_tiles(m, 3), rs_ref[m]))
        put(m, 0, SCALE * times_turned(fetch_tiles(m, 4), g_ref[m]))
        put(m, 3, half * times_turned(fetch_tiles(m, 5), rs_ref[m]))
        return carry

    def last_products(m, carry):
        put(m, 4, SCALE * times(fetch_tiles(m, 0), g_ref[m]))
        put(m, 2, half * times(fetch_tiles(m, 1), ps_ref[m]))
        return carry

    arrive(0)
    lax.fori_loop(0, count, first_products, 0)
    arrive(1)
    lax.fori_loop(0, count, last_products, 0)

    def close_up(pert, carry):
        to = pl.multiple_of(pert * message, message)
        one_ref[pl.ds(to, message), :] = two_ref[pl.ds(pert * stride, message), :]
        return carry

    leaves = []
    share = P_SIZE // store_sem.shape[0]
    for n in range(store_sem.shape[0]):
        lax.fori_loop(n * share, (n + 1) * share, close_up, 0)
        rows = pl.ds(n * share * message, share * message)
        leaves.append(pltpu.make_async_copy(one_ref.at[rows], out_ref.at[rows], store_sem.at[n]))
        leaves[n].start()
    for leave in leaves:
        leave.wait()

    for part in range(len(PARTS)):
        others = parts_ref[part].at[pl.ds(0, devices - 1)]
        pltpu.make_async_copy(others, others, send_sem.at[part]).wait()
    for n, (_, count, partners) in enumerate(steps):
        bytes_out = lists_ref.at[pl.ds(0, count * len(partners))]
        pltpu.make_async_copy(bytes_out, bytes_out, step_send.at[n]).wait()


def exchange(quartets, density, swap, integrals, devices):
    whole = pl.BlockSpec(memory_space=pltpu.VMEM)
    far = pl.BlockSpec(memory_space=pltpu.HBM)
    dma = pltpu.SemaphoreType.DMA
    spaced = pltpu.VMEM((devices * CHUNK + P_SIZE, LANES), f32)
    return pl.pallas_call(
        exchange_kernel,
        in_specs=[pl.BlockSpec(memory_space=pltpu.SMEM), far, far, far],
        out_specs=[whole, far],
        out_shape=[
            jax.ShapeDtypeStruct((SLOTS, devices), jnp.int32),
            jax.ShapeDtypeStruct((devices * CHUNK, LANES), f32),
        ],
        scratch_shapes=[
            pltpu.SMEM((1, 1, LANES), jnp.int32),
            pltpu.SMEM((devices, 1, LANES), jnp.int32),
            pltpu.VMEM((devices, 1, LANES), jnp.int32),
            pltpu.VMEM(density.shape, bf16),
            pltpu.VMEM(swap.shape, bf16),
            pltpu.VMEM((devices, CHUNK, LANES), bf16),
            pltpu.VMEM((devices, SUB * len(PARTS[0]), LANES), bf16),
            pltpu.VMEM((devices, SUB * len(PARTS[1]), LANES), bf16),
            pltpu.VMEM((NB * SPAN, SUB, LANES), f32),
            pltpu.VMEM(integrals.shape, bf16),
            pltpu.VMEM(integrals.shape, bf16),
            pltpu.VMEM(integrals.shape, bf16),
            pltpu.VMEM((S * (S + 1), LANES), f32),
            spaced,
            spaced,
            dma((4,)),
            dma((4,)),
            dma((4,)),
            dma((2,)),
            dma((2,)),
            dma((8,)),
        ],
        compiler_params=pltpu.CompilerParams(
            collective_id=0, has_side_effects=True, vmem_limit_bytes=EXCHANGE_VMEM
        ),
        name="exchange",
    )(quartets, density, swap, integrals)


def order_kernel(quartet_ref, made_ref, out_ref):
    message = QUARTERS * CHUNK
    perts = made_ref.shape[0] // message
    first = pl.program_id(0) * perts * message
    to = [
        [
            pl.multiple_of(first + quartet_ref[m, role] // SPAN * CHUNK, CHUNK)
            for role in range(3)
        ]
        for m in range(GROUP)
    ]
    for pert in range(perts):
        made = made_ref[message * pert : message * (pert + 1), :]
        for m in range(GROUP):
            for slot in range(SLOTS):
                at = m * CHUNK + slot * SUB
                rows = pl.ds(to[m][TILES[slot][0]] + (pert * message + slot * SUB), SUB)
                out_ref[rows, :] = made[at : at + SUB]


def by_owner(quartets, made):
    block = pl.BlockSpec((8 * QUARTERS * CHUNK, LANES), lambda i, quartets: (i, 0))
    return pl.pallas_call(
        order_kernel,
        grid_spec=pltpu.PrefetchScalarGridSpec(
            num_scalar_prefetch=1,
            grid=(P_SIZE // 8,),
            in_specs=[block],
            out_specs=pl.BlockSpec(memory_space=pltpu.VMEM),
        ),
        out_shape=jax.ShapeDtypeStruct(made.shape, f32),
        compiler_params=pltpu.CompilerParams(vmem_limit_bytes=46 << 20),
        name="by_owner",
    )(quartets, made)


def finish_kernel(index_ref, recv_ref, orb_ref, swap_ref, out_ref, sums_ref, rows_ref, fock_ref):
    chains = sums_ref.shape[0]

    def clear(n, carry):
        sums_ref[:, pl.ds(SPAN * n, SPAN)] = jnp.zeros((chains, SPAN, SUB, LANES), f32)
        return carry

    lax.fori_loop(0, NB, clear, 0)

    def one(e, carry):
        for turn in range(SLOTS // chains):
            slots = range(turn * chains, (turn + 1) * chains)
            at = [index_ref[slot, e] for slot in slots]
            new = [
                sums_ref[chain, at[chain]] + recv_ref[e, SUB * slot : SUB * (slot + 1), :]
                for chain, slot in enumerate(slots)
            ]
            for chain in range(chains):
                sums_ref[chain, at[chain]] = new[chain]
        return carry

    lax.fori_loop(0, recv_ref.shape[0], one, 0, unroll=4)

    wide = rows_ref.shape[0]

    def columns(c, carry):
        lefts = []
        for w in range(wide):
            parts = []
            for b in range(4):
                tiles = pl.ds((4 * (wide * c + w) + b) * SPAN, SPAN)
                total = sums_ref[0, tiles]
                for chain in range(1, chains):
                    total = total + sums_ref[chain, tiles]
                parts.append((total * (1.0 / SCALE)).astype(bf16).reshape(SPAN * SUB, LANES))
            lefts.append(jnp.concatenate(parts, axis=1))
        out = times(jnp.concatenate(lefts, axis=0), swap_ref[...])
        for w in range(wide):
            for s in range(4):
                rows_ref[w, pl.ds(s, LANES, stride=4), :] = out[
                    LANES * w : LANES * (w + 1), LANES * s : LANES * (s + 1)
                ]
            at = pl.multiple_of((wide * c + w) * LANES, LANES)
            fock_ref[:, pl.ds(at, LANES)] = rows_ref[w].astype(bf16)
        return carry

    lax.fori_loop(0, NB // 4 // wide, columns, 0)
    out_ref[...] = times(fock_ref[...], orb_ref[...])


def finish(index, arrived, orbitals, swap, rows):
    basis, occupied = orbitals.shape
    chains = 3
    whole = pl.BlockSpec(memory_space=pltpu.VMEM)
    return pl.pallas_call(
        finish_kernel,
        in_specs=[pl.BlockSpec(memory_space=pltpu.SMEM), whole, whole, whole],
        out_specs=whole,
        scratch_shapes=[
            pltpu.VMEM((chains, NB * SPAN, SUB, LANES), f32),
            pltpu.VMEM((4, rows, LANES), f32),
            pltpu.VMEM((rows, basis), bf16),
        ],
        out_shape=jax.ShapeDtypeStruct((rows, occupied), f32),
        compiler_params=pltpu.CompilerParams(vmem_limit_bytes=32 << 20),
        name="finish",
    )(index, arrived, orbitals, swap)


def per_device(integrals, quartets, density, orbitals):
    axes = ("quartet", "pert")
    devices = lax.axis_size("quartet") * lax.axis_size("pert")
    swap = group_swap()
    index, made = exchange(quartets, density, swap, integrals, devices)
    terms = by_owner(quartets, made)
    leaving = terms.astype(f16).reshape(devices, CHUNK, LANES)
    landed = lax.all_to_all(leaving, axes, 0, 0, tiled=True)
    return finish(index, landed.astype(f32), orbitals, swap, density.shape[0])


def solution(mesh):
    placed = (
        P(("quartet", "pert"), None, None),
        P(("quartet", "pert"), None),
        P(("quartet", "pert"), None),
        P(),
    )
    return jax.shard_map(
        per_device,
        mesh=mesh,
        in_specs=placed,
        out_specs=P(("quartet", "pert"), None),
        check_vma=False,
    )
```

```python
import jax
import jax.numpy as jnp
import numpy as np
from jax import lax
from jax.experimental import pallas as pl
from jax.experimental.pallas import tpu as pltpu
from jax.sharding import PartitionSpec as P

P_SIZE = 64
S = 32
NB = 64
QUARTERS = 4
PARTS = ((2, 3, 4, 5), (0, 1))
SPAN = NB // QUARTERS
GROUP = 4
SLOTS = 6
TILES = ((0, 1), (0, 2), (1, 3), (1, 2), (2, 3), (0, 3))
LANES = 128
SUB = 8
AREA = S * S
CHUNK = SLOTS * SUB
SCALE = 32.0

MESH = pl.DeviceIdType.MESH
EXCHANGE_VMEM = 54 << 20

f32 = jnp.float32
bf16 = jnp.bfloat16
f16 = jnp.float16


def group_swap():
    eye = np.eye(4 * LANES, dtype=np.float32)
    return jnp.asarray(eye.reshape(4, 4, S, 4 * LANES).transpose(1, 0, 2, 3).reshape(eye.shape), bf16)


def times(left, right):
    return jnp.dot(left, right, preferred_element_type=f32)


def times_turned(left, right):
    return lax.dot_general(left, right, (((1,), (1,)), ((), ())), preferred_element_type=f32)


def own_indices(quartet_ref, row_ref):
    members = [[quartet_ref[m, role] for role in range(4)] for m in range(GROUP)]
    for quarter in range(QUARTERS):
        low = quarter * SPAN

        def pick(row, column):
            total = jnp.int32(0)
            for member in members:
                within = jnp.logical_and(member[row] >= low, member[row] < low + SPAN)
                value = member[column] * SPAN + member[row] - low
                total = total + jnp.where(within, value, 0)
            return total

        for slot, (row, column) in enumerate(TILES):
            row_ref[0, 0, quarter * SLOTS + slot] = pick(row, column)
    for lane in range(QUARTERS * SLOTS, LANES):
        row_ref[0, 0, lane] = jnp.int32(0)


def exchange_kernel(
    quartet_ref,
    dens_from,
    swap_from,
    g_from,
    slots_ref,
    out_ref,
    row_ref,
    index_ref,
    lists_ref,
    dens_ref,
    swap_ref,
    message_ref,
    first_ref,
    last_ref,
    tiles_ref,
    g_ref,
    ps_ref,
    rs_ref,
    strip_ref,
    one_ref,
    two_ref,
    step_send,
    step_recv,
    own_sem,
    send_sem,
    recv_sem,
    store_sem,
):
    parts_ref = (first_ref, last_ref)
    chip, core = lax.axis_index("quartet"), lax.axis_index("pert")
    x, y, z = chip % 4, (chip // 4) % 4, chip // 16
    me = 2 * chip + core
    devices = lists_ref.shape[0]

    steps = (
        (me, 1, [(chip, (core + 1) % 2)]),
        (2 * chip, 2, [(chip - x + (x + n) % 4, core) for n in range(1, 4)]),
        (8 * (chip // 4), 8, [(chip - 4 * y + 4 * ((y + n) % 4), core) for n in range(1, 4)]),
        (32 * z, 32, [(chip - 16 * z + 16 * ((z + n) % 8), core) for n in range(1, 8)]),
    )
    barrier = pltpu.get_barrier_semaphore()
    for _, _, partners in steps:
        for partner in partners:
            pl.semaphore_signal(barrier, inc=1, device_id=partner, device_id_type=MESH)
    fetches = (
        pltpu.make_async_copy(dens_from, dens_ref, own_sem.at[1]),
        pltpu.make_async_copy(swap_from, swap_ref, own_sem.at[2]),
    )
    for fetch in fetches:
        fetch.start()
    g_load = pltpu.make_async_copy(g_from, g_ref, own_sem.at[3])
    own_indices(quartet_ref, row_ref)
    own = pltpu.make_async_copy(row_ref, lists_ref.at[pl.ds(me, 1)], own_sem.at[0])
    own.start()

    tall = dens_ref.shape[0]
    wide = dens_ref.shape[1] // LANES // len(steps)

    def cut(n):
        parts = []
        for w in range(wide):
            columns = slice(LANES * (wide * n + w), LANES * (wide * n + w + 1))
            one_ref[tall * w : tall * (w + 1), :] = dens_ref[:, columns].astype(f32)
            parts.append(
                jnp.concatenate(
                    [
                        one_ref[pl.ds(tall * w + s, LANES, stride=4), :].astype(bf16)
                        for s in range(4)
                    ],
                    axis=1,
                )
            )
        out = times(jnp.concatenate(parts, axis=0), swap_ref[...])
        for w in range(wide):
            for b in range(4):
                first = (4 * (wide * n + w) + b) * SPAN
                tiles_ref[first : first + SPAN] = out[
                    LANES * w : LANES * (w + 1), LANES * b : LANES * (b + 1)
                ].reshape(SPAN, SUB, LANES)

    own.wait()
    pl.semaphore_wait(barrier, sum(len(partners) for _, _, partners in steps))
    for n, (first, count, partners) in enumerate(steps):
        block = lists_ref.at[pl.ds(first, count)]
        for partner in partners:
            pltpu.make_async_remote_copy(
                src_ref=block,
                dst_ref=block,
                send_sem=step_send.at[n],
                recv_sem=step_recv.at[n],
                device_id=partner,
                device_id_type=MESH,
            ).start()
        if n == 0:
            for fetch in fetches:
                fetch.wait()
        cut(n)
        bytes_in = lists_ref.at[pl.ds(0, count * len(partners))]
        pltpu.make_async_copy(bytes_in, bytes_in, step_recv.at[n]).wait()

    to_scalars = pltpu.make_async_copy(lists_ref, index_ref, own_sem.at[0])
    to_scalars.start()
    g_load.start()
    to_scalars.wait()

    base = (me % QUARTERS) * SLOTS

    def pick(device, slots):
        for slot in slots[::2]:
            tiles = [tiles_ref[index_ref[device, 0, base + slot + half]] for half in range(2)]
            message_ref[device, SUB * slot : SUB * (slot + 2), :] = jnp.concatenate(
                tiles, axis=0
            ).astype(bf16)

    def send_part(part):
        slots = PARTS[part]
        rows = pl.ds(SUB * slots[0], SUB * len(slots))

        def send(n, carry):
            device = (me + n) % devices
            pick(device, slots)
            pltpu.make_async_remote_copy(
                src_ref=message_ref.at[device, rows],
                dst_ref=parts_ref[part].at[me],
                send_sem=send_sem.at[part],
                recv_sem=recv_sem.at[part],
                device_id=(device // 2, device % 2),
                device_id_type=MESH,
            ).start()
            return carry

        lax.fori_loop(1, devices, send, 0)
        pick(me, slots)
        pltpu.make_async_copy(
            message_ref.at[me, rows], parts_ref[part].at[me], own_sem.at[1 + part]
        ).start()

    for part in range(len(PARTS)):
        send_part(part)

    by_lane = lists_ref[...].reshape(devices, LANES).T
    slots = by_lane[:SLOTS]
    for quarter in range(1, QUARTERS):
        mine = by_lane[quarter * SLOTS : (quarter + 1) * SLOTS]
        slots = jnp.where(me % QUARTERS == quarter, mine, slots)
    slots_ref[...] = slots

    g_load.wait()
    count, area = g_ref.shape[0], g_ref.shape[1]
    strips = area // LANES
    gap = S + 1

    def strip(n, carry):
        m, step = n // strips, n % strips
        lanes = pl.ds(pl.multiple_of(step * LANES, LANES), LANES)
        swap = swap_ref[...]
        blocks = [g_ref[m, S * p : S * (p + 1), lanes] for p in range(S)]
        for p in range(S):
            strip_ref[gap * p : gap * p + S, :] = blocks[p].astype(f32)

        def spread(parts, target):
            out = times(jnp.concatenate(parts, axis=1), swap)
            for big in range(strips):
                for s in range(4):
                    first = gap * S * big + 4 * step + s
                    target[pl.ds(first, S, stride=gap), :] = out[
                        S * big : S * (big + 1), LANES * s : LANES * (s + 1)
                    ]

        spread(
            [
                jnp.concatenate(
                    [strip_ref[pl.ds(4 * big + r, S, stride=gap), :] for big in range(strips)],
                    axis=0,
                ).astype(bf16)
                for r in range(4)
            ],
            one_ref,
        )
        spread(
            [
                jnp.concatenate([blocks[4 * big + p] for big in range(strips)], axis=0)
                for p in range(4)
            ],
            two_ref,
        )

        @pl.when(step == strips - 1)
        def _():
            def close_up(big, carry):
                lanes = pl.ds(pl.multiple_of(big * LANES, LANES), LANES)
                for row in range(S):
                    first = gap * S * big + gap * row
                    rows = slice(S * row, S * (row + 1))
                    ps_ref[m, rows, lanes] = one_ref[pl.ds(first, S), :].astype(bf16)
                    rs_ref[m, rows, lanes] = two_ref[pl.ds(first, S), :].astype(bf16)
                return carry

            lax.fori_loop(0, strips, close_up, 0)

        return carry

    lax.fori_loop(0, count * strips, strip, 0)

    message = QUARTERS * CHUNK
    stride = message + 1
    quarters = [[quartet_ref[m, role] // SPAN for role in range(3)] for m in range(GROUP)]

    def arrive(part):
        rows = pl.ds(SUB * PARTS[part][0], SUB * len(PARTS[part]))
        pltpu.make_async_copy(
            message_ref.at[me, rows], parts_ref[part].at[me], own_sem.at[1 + part]
        ).wait()
        others = parts_ref[part].at[pl.ds(0, devices - 1)]
        pltpu.make_async_copy(others, others, recv_sem.at[part]).wait()

        def widen(pert, carry):
            for m in range(GROUP):
                for n, slot in enumerate(PARTS[part]):
                    device = QUARTERS * pert + quarters[m][TILES[slot][0]]
                    at = pert * stride + m * CHUNK + slot * SUB
                    one_ref[pl.ds(at, SUB), :] = parts_ref[part][
                        device, SUB * n : SUB * (n + 1), :
                    ].astype(f32)
            return carry

        lax.fori_loop(0, P_SIZE, widen, 0)

    def fetch_tiles(m, slot):
        first = m * CHUNK + slot * SUB
        return jnp.concatenate(
            [
                one_ref[pl.ds(first + c, P_SIZE, stride=stride), :].astype(bf16)
                for c in range(SUB)
            ],
            axis=1,
        )

    def put(m, slot, value):
        first = m * CHUNK + slot * SUB
        for c in range(SUB):
            two_ref[pl.ds(first + c, P_SIZE, stride=stride), :] = value[
                :, LANES * c : LANES * (c + 1)
            ]

    half = -0.5 * SCALE

    def first_products(m, carry):
        put(m, 1, half * times_turned(fetch_tiles(m, 2), ps_ref[m]))
        put(m, 5, half * times(fetch_tiles(m, 3), rs_ref[m]))
        put(m, 0, SCALE * times_turned(fetch_tiles(m, 4), g_ref[m]))
        put(m, 3, half * times_turned(fetch_tiles(m, 5), rs_ref[m]))
        return carry

    def last_products(m, carry):
        put(m, 4, SCALE * times(fetch_tiles(m, 0), g_ref[m]))
        put(m, 2, half * times(fetch_tiles(m, 1), ps_ref[m]))
        return carry

    arrive(0)
    lax.fori_loop(0, count, first_products, 0)
    arrive(1)
    lax.fori_loop(0, count, last_products, 0)

    def close_up(pert, carry):
        to = pl.multiple_of(pert * message, message)
        one_ref[pl.ds(to, message), :] = two_ref[pl.ds(pert * stride, message), :]
        return carry

    leaves = []
    share = P_SIZE // store_sem.shape[0]
    for n in range(store_sem.shape[0]):
        lax.fori_loop(n * share, (n + 1) * share, close_up, 0)
        rows = pl.ds(n * share * message, share * message)
        leaves.append(pltpu.make_async_copy(one_ref.at[rows], out_ref.at[rows], store_sem.at[n]))
        leaves[n].start()
    for leave in leaves:
        leave.wait()

    for part in range(len(PARTS)):
        others = parts_ref[part].at[pl.ds(0, devices - 1)]
        pltpu.make_async_copy(others, others, send_sem.at[part]).wait()
    for n, (_, count, partners) in enumerate(steps):
        bytes_out = lists_ref.at[pl.ds(0, count * len(partners))]
        pltpu.make_async_copy(bytes_out, bytes_out, step_send.at[n]).wait()


def exchange(quartets, density, swap, integrals, devices):
    whole = pl.BlockSpec(memory_space=pltpu.VMEM)
    far = pl.BlockSpec(memory_space=pltpu.HBM)
    dma = pltpu.SemaphoreType.DMA
    spaced = pltpu.VMEM((devices * CHUNK + P_SIZE, LANES), f32)
    return pl.pallas_call(
        exchange_kernel,
        in_specs=[pl.BlockSpec(memory_space=pltpu.SMEM), far, far, far],
        out_specs=[whole, far],
        out_shape=[
            jax.ShapeDtypeStruct((SLOTS, devices), jnp.int32),
            jax.ShapeDtypeStruct((devices * CHUNK, LANES), f32),
        ],
        scratch_shapes=[
            pltpu.SMEM((1, 1, LANES), jnp.int32),
            pltpu.SMEM((devices, 1, LANES), jnp.int32),
            pltpu.VMEM((devices, 1, LANES), jnp.int32),
            pltpu.VMEM(density.shape, bf16),
            pltpu.VMEM(swap.shape, bf16),
            pltpu.VMEM((devices, CHUNK, LANES), bf16),
            pltpu.VMEM((devices, SUB * len(PARTS[0]), LANES), bf16),
            pltpu.VMEM((devices, SUB * len(PARTS[1]), LANES), bf16),
            pltpu.VMEM((NB * SPAN, SUB, LANES), f32),
            pltpu.VMEM(integrals.shape, bf16),
            pltpu.VMEM(integrals.shape, bf16),
            pltpu.VMEM(integrals.shape, bf16),
            pltpu.VMEM((S * (S + 1), LANES), f32),
            spaced,
            spaced,
            dma((4,)),
            dma((4,)),
            dma((4,)),
            dma((2,)),
            dma((2,)),
            dma((8,)),
        ],
        compiler_params=pltpu.CompilerParams(
            collective_id=0, has_side_effects=True, vmem_limit_bytes=EXCHANGE_VMEM
        ),
        name="exchange",
    )(quartets, density, swap, integrals)


def order_kernel(quartet_ref, made_from, out_ref, made_ref, sem):
    message = QUARTERS * CHUNK
    shares = sem.shape[0]
    share = P_SIZE // shares
    loads = []
    for n in range(shares):
        rows = pl.ds(n * share * message, share * message)
        loads.append(pltpu.make_async_copy(made_from.at[rows], made_ref.at[rows], sem.at[n]))
        loads[n].start()
    to = [[quartet_ref[m, role] // SPAN * CHUNK for role in range(3)] for m in range(GROUP)]

    def one(pert, carry):
        first = pert * message
        for m in range(GROUP):
            for slot in range(SLOTS):
                at = pl.multiple_of(first + m * CHUNK + slot * SUB, SUB)
                there = pl.multiple_of(first + to[m][TILES[slot][0]] + slot * SUB, SUB)
                out_ref[pl.ds(there, SUB), :] = made_ref[pl.ds(at, SUB), :]
        return carry

    for n in range(shares):
        loads[n].wait()
        lax.fori_loop(n * share, (n + 1) * share, one, 0, unroll=2)


def by_owner(quartets, made):
    shares = 8
    return pl.pallas_call(
        order_kernel,
        in_specs=[
            pl.BlockSpec(memory_space=pltpu.SMEM),
            pl.BlockSpec(memory_space=pltpu.HBM),
        ],
        out_specs=pl.BlockSpec(memory_space=pltpu.VMEM),
        out_shape=jax.ShapeDtypeStruct(made.shape, f32),
        scratch_shapes=[pltpu.VMEM(made.shape, f32), pltpu.SemaphoreType.DMA((shares,))],
        compiler_params=pltpu.CompilerParams(vmem_limit_bytes=46 << 20),
        name="by_owner",
    )(quartets, made)


def finish_kernel(index_ref, recv_ref, orb_ref, swap_ref, out_ref, sums_ref, rows_ref, fock_ref):
    chains = sums_ref.shape[0]

    def clear(n, carry):
        sums_ref[:, pl.ds(SPAN * n, SPAN)] = jnp.zeros((chains, SPAN, SUB, LANES), f32)
        return carry

    lax.fori_loop(0, NB, clear, 0)

    def one(e, carry):
        for turn in range(SLOTS // chains):
            slots = range(turn * chains, (turn + 1) * chains)
            at = [index_ref[slot, e] for slot in slots]
            new = [
                sums_ref[chain, at[chain]] + recv_ref[e, SUB * slot : SUB * (slot + 1), :]
                for chain, slot in enumerate(slots)
            ]
            for chain in range(chains):
                sums_ref[chain, at[chain]] = new[chain]
        return carry

    lax.fori_loop(0, recv_ref.shape[0], one, 0, unroll=4)

    wide = rows_ref.shape[0]

    def columns(c, carry):
        lefts = []
        for w in range(wide):
            parts = []
            for b in range(4):
                tiles = pl.ds((4 * (wide * c + w) + b) * SPAN, SPAN)
                total = sums_ref[0, tiles]
                for chain in range(1, chains):
                    total = total + sums_ref[chain, tiles]
                parts.append((total * (1.0 / SCALE)).astype(bf16).reshape(SPAN * SUB, LANES))
            lefts.append(jnp.concatenate(parts, axis=1))
        out = times(jnp.concatenate(lefts, axis=0), swap_ref[...])
        for w in range(wide):
            for s in range(4):
                rows_ref[w, pl.ds(s, LANES, stride=4), :] = out[
                    LANES * w : LANES * (w + 1), LANES * s : LANES * (s + 1)
                ]
            at = pl.multiple_of((wide * c + w) * LANES, LANES)
            fock_ref[:, pl.ds(at, LANES)] = rows_ref[w].astype(bf16)
        return carry

    lax.fori_loop(0, NB // 4 // wide, columns, 0)
    out_ref[...] = times(fock_ref[...], orb_ref[...])


def finish(index, arrived, orbitals, swap, rows):
    basis, occupied = orbitals.shape
    chains = 3
    whole = pl.BlockSpec(memory_space=pltpu.VMEM)
    return pl.pallas_call(
        finish_kernel,
        in_specs=[pl.BlockSpec(memory_space=pltpu.SMEM), whole, whole, whole],
        out_specs=whole,
        scratch_shapes=[
            pltpu.VMEM((chains, NB * SPAN, SUB, LANES), f32),
            pltpu.VMEM((4, rows, LANES), f32),
            pltpu.VMEM((rows, basis), bf16),
        ],
        out_shape=jax.ShapeDtypeStruct((rows, occupied), f32),
        compiler_params=pltpu.CompilerParams(vmem_limit_bytes=32 << 20),
        name="finish",
    )(index, arrived, orbitals, swap)


def per_device(integrals, quartets, density, orbitals):
    axes = ("quartet", "pert")
    devices = lax.axis_size("quartet") * lax.axis_size("pert")
    swap = group_swap()
    index, made = exchange(quartets, density, swap, integrals, devices)
    terms = by_owner(quartets, made)
    leaving = terms.astype(f16).reshape(devices, CHUNK, LANES)
    landed = lax.all_to_all(leaving, axes, 0, 0, tiled=True)
    return finish(index, landed.astype(f32), orbitals, swap, density.shape[0])


def solution(mesh):
    placed = (
        P(("quartet", "pert"), None, None),
        P(("quartet", "pert"), None),
        P(("quartet", "pert"), None),
        P(),
    )
    return jax.shard_map(
        per_device,
        mesh=mesh,
        in_specs=placed,
        out_specs=P(("quartet", "pert"), None),
        check_vma=False,
    )
```
